768 devices in a mesh: seq: 96 (over x, z, core), grp: 8 (over y).
Axes of the slice: x: 4, y: 8, z: 12, core: 2. Of those that a mesh axis runs over, the one named last changes fastest.
Arguments:
- queries: bfloat16 [8, 12288, 1024], P('grp', 'seq'), may hold values from -6 to 6
- key_rows: bfloat16 [8, 12288, 1024], P('grp', 'seq'), may hold values from -6 to 6
- value_rows: bfloat16 [8, 12288, 1024], P('grp', 'seq'), may hold values from -6 to 6
- out_grad: bfloat16 [8, 12288, 1024], P('grp', 'seq'), may hold values from -6 to 6
- positions: int32 [8, 96], P('grp', 'seq'), may hold values from 0 to 2, as said below
- user_len: int32 [8, 96], P('grp', 'seq'), may hold values from 1 to 384, as said below
- position_bias: float32 [8, 384], replicated, may hold values from -3 to 3
Outputs:
- attended: bfloat16 [8, 12288, 1024], P('grp', 'seq')
- query_grad: bfloat16 [8, 12288, 1024], P('grp', 'seq')
- key_grad: bfloat16 [8, 12288, 1024], P('grp', 'seq')
- value_grad: bfloat16 [8, 12288, 1024], P('grp', 'seq')
- bias_grad: float32 [8, 384], replicated
The draws below stay inside these ranges and needn't reach their ends.
Inputs may be any that keep to these rules, and one draw needn't show every extreme that they name: `positions`: along seq within one grp index, histories occupy consecutive blocks numbered 0, 1, ... from the first; the first history of every group has exactly 3 blocks; no history has more than 3 blocks. `user_len`: equal on all blocks of one history; a history of b blocks has between (b - 1) * 128 + 1 and b * 128 events, so all its blocks but the last are full.
All inputs are finite; a program needn't handle non-finite values.
Results may differ from the reference program's by a relative error of at most 0.0053.
Values may be sent and summed in bfloat16 or wider, within the bound.
A program may use at most 32 MiB of HBM per device.

```python
import jax
import jax.numpy as jnp
from jax import lax

D = 1024
H = 8
BLOCK = 128
SPAN = 3
SEQ_ROWS = 12288
TABLE = 384
N_SEQ = 96
N_GRP = 8


def user_layout(key):
    count_key, fill_key = jax.random.split(key)
    device_index = jnp.arange(N_SEQ, dtype=jnp.int32)
    leading = device_index[None, :] == 0
    counts = jax.random.randint(count_key, (N_GRP, N_SEQ), 1, SPAN + 1).astype(jnp.int32)
    counts = jnp.where(leading, SPAN, counts)
    fills = jax.random.randint(fill_key, (N_GRP, N_SEQ), 1, BLOCK + 1).astype(jnp.int32)
    fills = jnp.where(leading, BLOCK, fills)
    ends = jnp.cumsum(counts, axis=1)
    starts = ends - counts
    owner = (starts[:, :, None] <= device_index[None, None, :]) & (ends[:, :, None] > device_index[None, None, :])
    kept = jnp.minimum(counts, N_SEQ - starts)
    start_of = jnp.sum(jnp.where(owner, starts[:, :, None], 0), axis=1)
    kept_of = jnp.sum(jnp.where(owner, kept[:, :, None], 0), axis=1)
    fill_of = jnp.sum(jnp.where(owner, fills[:, :, None], 0), axis=1)
    places = (device_index[None, :] - start_of).astype(jnp.int32)
    lengths = ((kept_of - 1) * BLOCK + fill_of).astype(jnp.int32)
    return (places, lengths)


def draw_positions(key, part):
    shared = user_layout(key)
    return shared[0]


def draw_user_len(key, part):
    shared = user_layout(key)
    return shared[1]


def shard_levels(own_key, extent, cuts, least, largest):
    factor_of, own = 1.0, jax.random.fold_in(own_key, 6)
    for position, shards_of in cuts:
        draws = jnp.exp(jax.random.uniform(jax.random.fold_in(own, position), (shards_of,), jnp.float32, least / len(cuts), largest / len(cuts)))
        factor_of = factor_of * jnp.repeat(draws, extent[position] // shards_of).reshape([-1 if axis == position else 1 for axis in range(len(extent))])
    return factor_of


def centred(rng, extent, deviation, limit, cuts=(), held_as=jnp.bfloat16):
    level = shard_levels(rng, extent, cuts, -0.22, 0.18) if cuts else 1.0
    array = jax.random.normal(rng, extent, jnp.float32) * deviation * level
    return jnp.minimum(jnp.maximum(array, -limit), limit).astype(held_as)


def setup_inputs(seed: int = 0) -> dict:
    key_of = jax.random.split(jax.random.key(seed), 8)
    return {
        "queries": centred(key_of[0], (N_GRP, SEQ_ROWS, D), 1.0, 6.0, ((0, 8), (1, 96))),
        "key_rows": centred(key_of[1], (N_GRP, SEQ_ROWS, D), 1.0, 6.0, ((0, 8), (1, 96))),
        "value_rows": centred(key_of[2], (N_GRP, SEQ_ROWS, D), 1.0, 6.0, ((0, 8), (1, 96))),
        "out_grad": centred(key_of[3], (N_GRP, SEQ_ROWS, D), 1.0, 6.0, ((0, 8), (1, 96))),
        "positions": draw_positions(jax.random.fold_in(key_of[7], 71), 0),
        "user_len": draw_user_len(jax.random.fold_in(key_of[7], 71), 0),
        "position_bias": centred(key_of[6], (H, TABLE), 0.5, 3.0, (), jnp.float32),
    }


def settle(values):
    return lax.optimization_barrier(values.astype(jnp.bfloat16)).astype(jnp.float32)


def block_pair(query_blk, key_blk, value_blk, grad_blk, offset, rows_valid, length, position_bias, active):
    head_dim = D // H
    score_scale = head_dim ** -0.5

    def compute(unused):
        row_index = jnp.arange(BLOCK, dtype=jnp.int32)
        distance = offset * BLOCK + row_index[:, None] - row_index[None, :]
        usable = ((distance >= 0) & (row_index[:, None] < rows_valid))[None]
        clipped = jnp.clip(distance, 0, SPAN * BLOCK - 1).astype(jnp.int32)
        near = position_bias[:, clipped]
        query_heads = query_blk.astype(jnp.float32).reshape(BLOCK, H, head_dim)
        key_heads = key_blk.astype(jnp.float32).reshape(BLOCK, H, head_dim)
        value_heads = value_blk.astype(jnp.float32).reshape(BLOCK, H, head_dim)
        grad_heads = grad_blk.astype(jnp.float32).reshape(BLOCK, H, head_dim)
        scores = jnp.einsum("rhd,chd->hrc", query_heads, key_heads) * score_scale + near
        sigmoid_part = jax.nn.sigmoid(scores)
        inverse = 1.0 / length.astype(jnp.float32)
        weights = settle(jnp.where(usable, scores * sigmoid_part * inverse, 0.0))
        attended = jnp.einsum("hrc,chd->rhd", weights, value_heads).reshape(BLOCK, D)
        pulled = jnp.einsum("rhd,chd->hrc", grad_heads, value_heads)
        slopes = jnp.where(usable, pulled * sigmoid_part * (1.0 + scores * (1.0 - sigmoid_part)) * inverse, 0.0)
        slopes_low = settle(slopes)
        query_grad = jnp.einsum("hrc,chd->rhd", slopes_low, key_heads).reshape(BLOCK, D) * score_scale
        key_grad = jnp.einsum("hrc,rhd->chd", slopes_low, query_heads).reshape(BLOCK, D) * score_scale
        value_grad = jnp.einsum("hrc,rhd->chd", weights, grad_heads).reshape(BLOCK, D)
        bias_part = jnp.zeros((H, SPAN * BLOCK), jnp.float32).at[:, clipped].add(slopes)
        return attended, query_grad, key_grad, value_grad, bias_part

    def skipped(unused):
        empty = jnp.zeros((BLOCK, D), jnp.float32)
        return empty, empty, empty, empty, jnp.zeros((H, SPAN * BLOCK), jnp.float32)

    return lax.cond(active, compute, skipped, None)


def reference(queries, key_rows, value_rows, out_grad, positions, user_len, position_bias):
    shape_four = (N_GRP, N_SEQ, BLOCK, D)
    query_four = queries.reshape(shape_four)
    key_four = key_rows.reshape(shape_four)
    value_four = value_rows.reshape(shape_four)
    grad_four = out_grad.reshape(shape_four)
    place_flat = positions.reshape(-1).astype(jnp.int32)
    length_flat = user_len.reshape(-1).astype(jnp.int32)
    valid_flat = jnp.clip(length_flat - place_flat * BLOCK, 0, BLOCK).astype(jnp.int32)
    totals = [jnp.zeros(shape_four, jnp.float32) for unused in range(4)]
    bias_total = jnp.zeros((H, SPAN * BLOCK), jnp.float32)
    for offset in range(SPAN):
        pad_spec = ((0, 0), (offset, 0), (0, 0), (0, 0))
        key_moved = jnp.pad(key_four, pad_spec)[:, :N_SEQ].reshape(N_GRP * N_SEQ, BLOCK, D)
        value_moved = jnp.pad(value_four, pad_spec)[:, :N_SEQ].reshape(N_GRP * N_SEQ, BLOCK, D)
        active_flat = place_flat >= offset

        def per_block(items):
            terms = block_pair(items[0], items[1], items[2], items[3], offset, items[4], items[5], position_bias, items[6])
            if offset > 0:
                return tuple(term.astype(jnp.bfloat16) for term in terms[:4]) + (terms[4],)
            return terms

        terms = lax.map(per_block, (query_four.reshape(-1, BLOCK, D), key_moved, value_moved, grad_four.reshape(-1, BLOCK, D), valid_flat, length_flat, active_flat))
        parts = [term.astype(jnp.float32).reshape(shape_four) for term in terms[:4]]
        back_spec = ((0, 0), (0, offset), (0, 0), (0, 0))
        totals[0] = totals[0] + parts[0]
        totals[1] = totals[1] + parts[1]
        totals[2] = totals[2] + jnp.pad(parts[2][:, offset:], back_spec)
        totals[3] = totals[3] + jnp.pad(parts[3][:, offset:], back_spec)
        bias_total = bias_total + jnp.sum(terms[4], axis=0)
    outputs = tuple(total.reshape(N_GRP, N_SEQ * BLOCK, D).astype(jnp.bfloat16) for total in totals)
    bias_grad = bias_total * (N_SEQ * N_GRP) ** -0.5
    return outputs[0], outputs[1], outputs[2], outputs[3], bias_grad
```

```python
import jax
import jax.numpy as jnp
from jax import lax
from jax.experimental import pallas as pl
from jax.experimental.pallas import tpu as pltpu
from jax.sharding import PartitionSpec as P

H = 8
BLOCK = 128
D = 1024
MESH = pl.DeviceIdType.MESH
F32 = jnp.float32
BF16 = jnp.bfloat16
SCALE = 128 ** -0.5


def own_row(side):
    return pl.multiple_of(256 * (1 - side), 128)


def far_row(side):
    return pl.multiple_of(256 * side, 128)


def head_cols(h):
    return pl.ds(pl.multiple_of(h * 128, 128), 128)


def flip(x):
    lane = lax.broadcasted_iota(jnp.int32, x.shape, 1)
    return jnp.take_along_axis(x, 127 - lane, axis=1, mode="promise_in_bounds")


def skew(x, left):
    width = x.shape[1]
    row = lax.broadcasted_iota(jnp.int32, x.shape, 0)
    for bit in (1, 2, 4):
        moved = pltpu.roll(x, width - bit if left else bit, 1)
        x = jnp.where((row & bit) != 0, moved, x)
    return x


def nt(a, b):
    return lax.dot_general(a, b, (((1,), (1,)), ((), ())), preferred_element_type=F32)


def diagonals(slopes, width):
    total = None
    for i in range(16):
        slab = slopes[8 * i : 8 * i + 8]
        if i:
            slab = pltpu.roll(slab, width - 8 * i, 1)
        total = slab if total is None else total + slab
    return skew(total, True)


def main_kernel(
    q_ref, k_ref, v_ref, g_ref, pos_ref, len_ref, bias_ref,
    res_ref, bg_ref,
    wide, toep, mask, outb, acc, bl, r1, r2, fin,
    load_sem, chip_send, chip_recv, w1_send, w1_recv, rel_send, rel_recv, w2_send, w2_recv,
    ar_send, ar_recv, out_sem,
):
    s = lax.axis_index("seq")
    grp = lax.axis_index("grp")
    n_seq = lax.axis_size("seq")
    n_grp = lax.axis_size("grp")
    c = s % 2
    x = s // 24
    m = s % 24
    d = 1 - c
    e = c
    sib = {"seq": s + 1 - 2 * c, "grp": grp}
    ahead = {"seq": (s + 4 * c - 2 + n_seq) % n_seq, "grp": grp}
    behind = {"seq": (s + 2 - 4 * c + n_seq) % n_seq, "grp": grp}

    loads = []
    for i, (ref, side, part) in enumerate(
        ((q_ref, 1, 0), (g_ref, 1, 1), (k_ref, 0, 0), (v_ref, 0, 1))
    ):
        row = 256 * (1 - side)
        copy = pltpu.make_async_copy(
            ref.at[0], wide.at[side, part, pl.ds(row, 128)], load_sem.at[i]
        )
        copy.start()
        loads.append(copy)

    barrier = pltpu.get_barrier_semaphore()

    def greet(device):
        pl.semaphore_signal(barrier, inc=1, device_id=device, device_id_type=MESH)

    def line_peer(j):
        return {"seq": x * 24 + (m + j) % 24, "grp": grp}

    def plane_peer(j):
        t = (x * n_grp + grp + j) % 32
        return {"seq": (t // n_grp) * 24 + m, "grp": t % n_grp}

    greet(ahead)
    greet(behind)

    def greet_line(j, carry):
        greet(line_peer(j))
        return carry

    def greet_plane(j, carry):
        greet(plane_peer(j))
        return carry

    lax.fori_loop(1, 24, greet_line, 0)
    lax.fori_loop(1, 32, greet_plane, 0)

    p = pos_ref[0, 0]
    n = len_ref[0, 0]
    row = lax.broadcasted_iota(jnp.int32, (128, 384), 0)
    lane = lax.broadcasted_iota(jnp.int32, (128, 384), 1)
    inverse = 1.0 / jnp.full((128, 384), n, jnp.int32).astype(F32)
    used = (row < n - p * 128) & (lane >= 256 - 128 * p) & (lane <= 256 + row)
    mask[0] = jnp.where(used, inverse, 0.0)
    used = (lane < n - p * 128) & (lane >= row)
    mask[1] = jnp.where(used, inverse, 0.0)

    def make_toep(h, carry):
        b = jnp.broadcast_to(bias_ref[pl.ds(h, 1), :] * 0.5, (8, 384))
        b0, b1, b2 = b[:, :128], b[:, 128:256], b[:, 256:]
        zero = jnp.zeros_like(b0)
        keyed = skew(jnp.concatenate([b0, b1, b2, zero], axis=1), False)
        quer = jnp.concatenate([flip(b1), flip(b0), zero, flip(b2)], axis=1)
        quer = skew(pltpu.roll(quer, 1, 1), False)
        for i in range(16):
            toep[1, h, 8 * i : 8 * i + 8, :] = (pltpu.roll(keyed, 8 * i, 1) if i else keyed)[:, :384]
            toep[0, h, 8 * i : 8 * i + 8, :] = (pltpu.roll(quer, 8 * i, 1) if i else quer)[:, :384]
        return carry

    lax.fori_loop(0, H, make_toep, 0)

    for copy in loads:
        copy.wait()
    pl.semaphore_wait(barrier, 2 + 23 + 31)

    def piece(side, part, rows, h):
        return wide.at[side, part, pl.ds(rows, 128), head_cols(h)]

    def first_copy(h, part):
        return pltpu.make_async_remote_copy(
            src_ref=piece(d, part, own_row(d), h), dst_ref=piece(d, part, far_row(d), h),
            send_sem=w1_send.at[h, part], recv_sem=w1_recv.at[h, part],
            device_id=ahead, device_id_type=MESH,
        )

    def second_copy(h, part):
        return pltpu.make_async_remote_copy(
            src_ref=piece(e, part, own_row(e), h), dst_ref=piece(e, part, far_row(e), h),
            send_sem=w2_send.at[h, part], recv_sem=w2_recv.at[h, part],
            device_id=behind, device_id_type=MESH,
        )

    def relay_copy(h, part):
        return pltpu.make_async_remote_copy(
            src_ref=piece(d, part, far_row(d), h), dst_ref=piece(d, part, 128, h),
            send_sem=rel_send.at[h, part], recv_sem=rel_recv.at[h, part],
            device_id=sib, device_id_type=MESH,
        )

    def chip_copy(part):
        return pltpu.make_async_remote_copy(
            src_ref=wide.at[e, part, pl.ds(own_row(e), 128)],
            dst_ref=wide.at[e, part, pl.ds(128, 128)],
            send_sem=chip_send.at[part], recv_sem=chip_recv.at[part],
            device_id=sib, device_id_type=MESH,
        )

    def start_first(h, carry):
        first_copy(h, 0).start()
        first_copy(h, 1).start()
        return carry

    lax.fori_loop(0, H, start_first, 0)
    chip_copy(0).start()
    chip_copy(1).start()

    def block(side, h, lo, width):
        cols = head_cols(h)
        rows = pl.ds(lo, width)
        other = 1 - side
        own = pl.ds(own_row(other), 128)
        x3 = wide[side, 0, rows, cols]
        y3 = wide[side, 1, rows, cols]
        y = nt(wide[other, 0, own, cols], x3) * (0.5 * SCALE) + toep[side, h, :, rows]
        pulled = nt(wide[other, 1, own, cols], y3)
        t = jnp.tanh(y)
        w0 = y * t + y
        sg = 0.5 * t + 0.5
        mk = mask[side, :, rows]
        weights = (w0 * mk).astype(BF16)
        slopes = pulled * (sg + w0 * (1.0 - sg)) * mk
        o1 = jnp.dot(weights, y3, preferred_element_type=F32)
        o2 = jnp.dot(slopes.astype(BF16), x3, preferred_element_type=F32) * SCALE
        return o1, o2, slopes

    chip_copy(0).wait_recv()
    chip_copy(1).wait_recv()

    def other_near(h):
        relay_copy(h, 0).wait_recv()
        relay_copy(h, 1).wait_recv()
        o1, o2, slopes = block(e, h, pl.multiple_of(128 * (1 - e), 128), 256)
        acc[0, :, head_cols(h)] = o1
        acc[1, :, head_cols(h)] = o2

        @pl.when(c == 1)
        def _():
            near = slopes[:, 128:256]
            diag = diagonals(jnp.concatenate([jnp.zeros_like(near), near], axis=1), 256)
            total = jnp.sum(diag, axis=0, keepdims=True)
            bl[3 * h] = bl[3 * h] + total[:, :128]
            bl[3 * h + 1] = bl[3 * h + 1] + total[:, 128:]

    keep_near = jnp.where(c == 0, 1.0, 0.0).astype(F32)

    def direct(h, carry):
        for part in range(2):
            first_copy(h, part).wait_recv()
            relay_copy(h, part).start()
        o1, o2, slopes = block(d, h, 0, 384)
        outb[d, 0, :, head_cols(h)] = o1.astype(BF16)
        outb[d, 1, :, head_cols(h)] = o2.astype(BF16)
        framed = jnp.concatenate(
            [slopes[:, :128], slopes[:, 128:256] * keep_near, slopes[:, 256:], jnp.zeros((128, 128), F32)],
            axis=1,
        )
        diag = diagonals(framed, 512)
        back = pltpu.roll(diag, 511, 1)
        source = (1, 0, 3)
        for k in range(3):
            straight = diag[:, 128 * k : 128 * k + 128]
            turned = flip(back[:, 128 * source[k] : 128 * source[k] + 128])
            total = jnp.where(jnp.full((8, 128), c) == 0, straight, turned)
            bl[3 * h + k] = jnp.sum(total, axis=0, keepdims=True)

        @pl.when(h > 0)
        def _():
            other_near(h - 1)

        return carry

    lax.fori_loop(0, H, direct, 0)

    def start_second(h, carry):
        for part in range(2):
            first_copy(h, part).wait_send()
            second_copy(h, part).start()
        return carry

    lax.fori_loop(0, H, start_second, 0)
    direct_out = pltpu.make_async_copy(outb.at[d], res_ref.at[d], out_sem.at[0])
    direct_out.start()
    other_near(H - 1)

    def ar_copy(step, src, dst, device):
        return pltpu.make_async_remote_copy(
            src_ref=src, dst_ref=dst, send_sem=ar_send.at[step], recv_sem=ar_recv.at[step],
            device_id=device, device_id_type=MESH,
        )

    def finish(lo, hi):
        def body(h, carry):
            for part in range(2):
                second_copy(h, part).wait_recv()
            o1, o2, _ = block(e, h, far_row(e), 128)
            outb[e, 0, :, head_cols(h)] = (acc[0, :, head_cols(h)] + o1).astype(BF16)
            outb[e, 1, :, head_cols(h)] = (acc[1, :, head_cols(h)] + o2).astype(BF16)
            return carry

        lax.fori_loop(lo, hi, body, 0)

    def send_rows(j, carry):
        k = (m + j) % 24
        ar_copy(0, bl.at[k], r1.at[m], line_peer(j)).start()
        return carry

    lax.fori_loop(1, 24, send_rows, 0)
    r1[m] = bl[m]
    finish(0, 2)
    ar_copy(0, bl.at[pl.ds(0, 23)], r1.at[pl.ds(0, 23)], sib).wait()
    me = x * n_grp + grp
    r2[me] = jnp.sum(r1[...], axis=0)

    def send_sums(j, carry):
        ar_copy(1, r2.at[me], r2.at[me], plane_peer(j)).start()
        return carry

    lax.fori_loop(1, 32, send_sums, 0)
    finish(2, 5)
    ar_copy(1, r2.at[pl.ds(0, 31)], r2.at[pl.ds(0, 31)], sib).wait()
    fin[m] = jnp.sum(r2[...], axis=0) * (n_seq * n_grp) ** (-0.5)

    def send_done(j, carry):
        ar_copy(2, fin.at[m], fin.at[m], line_peer(j)).start()
        return carry

    lax.fori_loop(1, 24, send_done, 0)
    finish(5, H)
    other_out = pltpu.make_async_copy(outb.at[e], res_ref.at[e], out_sem.at[1])
    other_out.start()
    ar_copy(2, fin.at[pl.ds(0, 23)], fin.at[pl.ds(0, 23)], sib).wait()
    for h in range(H):
        for k in range(3):
            bg_ref[h : h + 1, 128 * k : 128 * k + 128] = fin[3 * h + k]

    for part in range(2):
        chip_copy(part).wait_send()

    def drain(h, carry):
        for part in range(2):
            relay_copy(h, part).wait_send()
            second_copy(h, part).wait_send()
        return carry

    lax.fori_loop(0, H, drain, 0)
    direct_out.wait()
    other_out.wait()


def copy_kernel(res_ref, bg_ref, att_ref, qg_ref, kg_ref, vg_ref, bias_ref, sem):
    copies = []
    for i, (side, part, ref) in enumerate(
        ((0, 0, att_ref), (0, 1, qg_ref), (1, 1, kg_ref), (1, 0, vg_ref))
    ):
        copy = pltpu.make_async_copy(res_ref.at[side, part], ref.at[0], sem.at[i])
        copy.start()
        copies.append(copy)
    bias_ref[...] = bg_ref[...]
    for copy in copies:
        copy.wait()


def on_device(queries, key_rows, value_rows, out_grad, positions, user_len, position_bias):
    any_spec = pl.BlockSpec(memory_space=pl.ANY)
    vmem = pl.BlockSpec(memory_space=pltpu.VMEM)
    smem = pl.BlockSpec(memory_space=pltpu.SMEM)
    dma = pltpu.SemaphoreType.DMA
    res, bg = pl.pallas_call(
        main_kernel,
        out_shape=(
            jax.ShapeDtypeStruct((2, 2, BLOCK, D), BF16),
            jax.ShapeDtypeStruct((H, 384), F32),
        ),
        in_specs=[any_spec] * 4 + [smem, smem, vmem],
        out_specs=(any_spec, vmem),
        scratch_shapes=[
            pltpu.VMEM((2, 2, 384, D), BF16),
            pltpu.VMEM((2, H, 128, 384), F32),
            pltpu.VMEM((2, 128, 384), F32),
            pltpu.VMEM((2, 2, 128, D), BF16),
            pltpu.VMEM((2, 128, D), F32),
            pltpu.VMEM((24, 1, 128), F32),
            pltpu.VMEM((24, 1, 128), F32),
            pltpu.VMEM((32, 1, 128), F32),
            pltpu.VMEM((24, 1, 128), F32),
            dma((4,)),
            dma((2,)),
            dma((2,)),
            dma((H, 2)),
            dma((H, 2)),
            dma((H, 2)),
            dma((H, 2)),
            dma((H, 2)),
            dma((H, 2)),
            dma((3,)),
            dma((3,)),
            dma((2,)),
        ],
        compiler_params=pltpu.CompilerParams(
            collective_id=0, has_side_effects=True, vmem_limit_bytes=48 * 1024 * 1024
        ),
        name="attention",
    )(queries, key_rows, value_rows, out_grad, positions, user_len, position_bias)
    whole = jax.ShapeDtypeStruct((1, BLOCK, D), BF16)
    return pl.pallas_call(
        copy_kernel,
        out_shape=(whole, whole, whole, whole, jax.ShapeDtypeStruct((H, 384), F32)),
        in_specs=[any_spec, vmem],
        out_specs=(any_spec, any_spec, any_spec, any_spec, vmem),
        scratch_shapes=[dma((4,))],
        name="results",
    )(res, bg)


def solution(mesh):
    return jax.shard_map(
        on_device,
        mesh=mesh,
        in_specs=(
            P("grp", "seq", None),
            P("grp", "seq", None),
            P("grp", "seq", None),
            P("grp", "seq", None),
            P("grp", "seq"),
            P("grp", "seq"),
            P(),
        ),
        out_specs=(
            P("grp", "seq", None),
            P("grp", "seq", None),
            P("grp", "seq", None),
            P("grp", "seq", None),
            P(),
        ),
        check_vma=False,
    )
```

```python
import jax
import jax.numpy as jnp
from jax import lax
from jax.experimental import pallas as pl
from jax.experimental.pallas import tpu as pltpu
from jax.sharding import PartitionSpec as P

H = 8
BLOCK = 128
D = 1024
MESH = pl.DeviceIdType.MESH
F32 = jnp.float32
BF16 = jnp.bfloat16
SCALE = 128 ** -0.5


def own_row(side):
    return pl.multiple_of(256 * (1 - side), 128)


def far_row(side):
    return pl.multiple_of(256 * side, 128)


def head_cols(h):
    return pl.ds(pl.multiple_of(h * 128, 128), 128)


def flip(x):
    lane = lax.broadcasted_iota(jnp.int32, x.shape, 1)
    return jnp.take_along_axis(x, 127 - lane, axis=1, mode="promise_in_bounds")


def skew(x, left):
    width = x.shape[1]
    row = lax.broadcasted_iota(jnp.int32, x.shape, 0)
    for bit in (1, 2, 4):
        moved = pltpu.roll(x, width - bit if left else bit, 1)
        x = jnp.where((row & bit) != 0, moved, x)
    return x


def nt(a, b):
    return lax.dot_general(a, b, (((1,), (1,)), ((), ())), preferred_element_type=F32)


def diagonals(slopes, width):
    total = None
    for i in range(16):
        slab = slopes[8 * i : 8 * i + 8]
        if i:
            slab = pltpu.roll(slab, width - 8 * i, 1)
        total = slab if total is None else total + slab
    return skew(total, True)


def main_kernel(
    q_ref, k_ref, v_ref, g_ref, pos_ref, len_ref, bias_ref,
    res_ref, bg_ref,
    wide, toep, mask, bias, place, acc, bl, r1, r2, fin,
    load_sem, chip_send, chip_recv, w1_send, w1_recv, rel_send, rel_recv, w2_send, w2_recv,
    up_send, up_recv, flat_send, flat_recv, down_send, down_recv, small_sem,
):
    s = lax.axis_index("seq")
    grp = lax.axis_index("grp")
    n_seq = lax.axis_size("seq")
    n_grp = lax.axis_size("grp")
    c = s % 2
    x = s // 24
    m = s % 24
    d = 1 - c
    e = c
    sib = {"seq": s + 1 - 2 * c, "grp": grp}
    ahead = {"seq": (s + 4 * c - 2 + n_seq) % n_seq, "grp": grp}
    behind = {"seq": (s + 2 - 4 * c + n_seq) % n_seq, "grp": grp}

    smalls = []
    for i, (src, dst) in enumerate(
        ((bias_ref, bias), (pos_ref, place.at[pl.ds(0, 1)]), (len_ref, place.at[pl.ds(1, 1)]))
    ):
        copy = pltpu.make_async_copy(src, dst, small_sem.at[i])
        copy.start()
        smalls.append(copy)
    loads = []
    for i, (ref, side, part) in enumerate(
        ((q_ref, 1, 0), (g_ref, 1, 1), (k_ref, 0, 0), (v_ref, 0, 1))
    ):
        row = 256 * (1 - side)
        copy = pltpu.make_async_copy(
            ref.at[0], wide.at[side, part, pl.ds(row, 128)], load_sem.at[i]
        )
        copy.start()
        loads.append(copy)

    barrier = pltpu.get_barrier_semaphore()

    def greet(device):
        pl.semaphore_signal(barrier, inc=1, device_id=device, device_id_type=MESH)

    def line_peer(j):
        return {"seq": s - m + j, "grp": grp}

    def plane_peer(j):
        t = (x * n_grp + grp + j) % 32
        return {"seq": (t // n_grp) * 24 + m, "grp": t % n_grp}

    adds = m < 2
    greet(ahead)
    greet(behind)
    greet(sib)

    @pl.when(adds)
    def _():
        for j in range(1, 32):
            greet(plane_peer(j))
        for j in range(2, 24):
            greet(line_peer(j))

    for copy in loads:
        copy.wait()

    @pl.when(adds)
    def _():
        pl.semaphore_wait(barrier, 3 + 31)

    @pl.when(jnp.logical_not(adds))
    def _():
        pl.semaphore_wait(barrier, 3 + 2)

    def piece(side, part, rows, h):
        return wide.at[side, part, pl.ds(rows, 128), head_cols(h)]

    def first_copy(h, part):
        return pltpu.make_async_remote_copy(
            src_ref=piece(d, part, own_row(d), h), dst_ref=piece(d, part, far_row(d), h),
            send_sem=w1_send.at[h, part], recv_sem=w1_recv.at[h, part],
            device_id=ahead, device_id_type=MESH,
        )

    def second_copy(h, part):
        return pltpu.make_async_remote_copy(
            src_ref=piece(e, part, own_row(e), h), dst_ref=piece(e, part, far_row(e), h),
            send_sem=w2_send.at[h, part], recv_sem=w2_recv.at[h, part],
            device_id=behind, device_id_type=MESH,
        )

    def relay_copy(h, part):
        return pltpu.make_async_remote_copy(
            src_ref=piece(d, part, far_row(d), h), dst_ref=piece(d, part, 128, h),
            send_sem=rel_send.at[h, part], recv_sem=rel_recv.at[h, part],
            device_id=sib, device_id_type=MESH,
        )

    def chip_copy(part):
        return pltpu.make_async_remote_copy(
            src_ref=wide.at[e, part, pl.ds(own_row(e), 128)],
            dst_ref=wide.at[e, part, pl.ds(128, 128)],
            send_sem=chip_send.at[part], recv_sem=chip_recv.at[part],
            device_id=sib, device_id_type=MESH,
        )

    def start_first(h, carry):
        first_copy(h, 0).start()
        first_copy(h, 1).start()
        return carry

    lax.fori_loop(0, H, start_first, 0)
    chip_copy(0).start()
    chip_copy(1).start()

    for copy in smalls:
        copy.wait()
    p = place[0, 0]
    n = place[1, 0]
    row = lax.broadcasted_iota(jnp.int32, (128, 384), 0)
    lane = lax.broadcasted_iota(jnp.int32, (128, 384), 1)
    inverse = 1.0 / jnp.full((128, 384), n, jnp.int32).astype(F32)
    used = (row < n - p * 128) & (lane >= 256 - 128 * p) & (lane <= 256 + row)
    mask[0] = jnp.where(used, inverse, 0.0)
    used = (lane < n - p * 128) & (lane >= row)
    mask[1] = jnp.where(used, inverse, 0.0)

    def make_toep(h, carry):
        b = jnp.broadcast_to(bias[pl.ds(h, 1), :] * 0.5, (8, 384))
        b0, b1, b2 = b[:, :128], b[:, 128:256], b[:, 256:]
        zero = jnp.zeros_like(b0)
        keyed = skew(jnp.concatenate([b0, b1, b2, zero], axis=1), False)
        quer = jnp.concatenate([flip(b1), flip(b0), zero, flip(b2)], axis=1)
        quer = skew(pltpu.roll(quer, 1, 1), False)
        for i in range(16):
            toep[1, h, 8 * i : 8 * i + 8, :] = (pltpu.roll(keyed, 8 * i, 1) if i else keyed)[:, :384]
            toep[0, h, 8 * i : 8 * i + 8, :] = (pltpu.roll(quer, 8 * i, 1) if i else quer)[:, :384]
        return carry

    lax.fori_loop(0, H, make_toep, 0)

    def block(side, h, lo, width):
        cols = head_cols(h)
        rows = pl.ds(lo, width)
        other = 1 - side
        own = pl.ds(own_row(other), 128)
        x3 = wide[side, 0, rows, cols]
        y3 = wide[side, 1, rows, cols]
        y = nt(wide[other, 0, own, cols], x3) * (0.5 * SCALE) + toep[side, h, :, rows]
        pulled = nt(wide[other, 1, own, cols], y3)
        t = jnp.tanh(y)
        w0 = y * t + y
        sg = 0.5 * t + 0.5
        mk = mask[side, :, rows]
        weights = (w0 * mk).astype(BF16)
        slopes = pulled * (sg + w0 * (1.0 - sg)) * mk
        o1 = jnp.dot(weights, y3, preferred_element_type=F32)
        o2 = jnp.dot(slopes.astype(BF16), x3, preferred_element_type=F32) * SCALE
        return o1, o2, slopes

    chip_copy(0).wait_recv()
    chip_copy(1).wait_recv()

    def other_near(h):
        relay_copy(h, 0).wait_recv()
        relay_copy(h, 1).wait_recv()
        o1, o2, slopes = block(e, h, pl.multiple_of(128 * (1 - e), 128), 256)
        acc[0, :, head_cols(h)] = o1
        acc[1, :, head_cols(h)] = o2

        @pl.when(c == 1)
        def _():
            near = slopes[:, 128:256]
            diag = diagonals(jnp.concatenate([jnp.zeros_like(near), near], axis=1), 256)
            total = jnp.sum(diag, axis=0, keepdims=True)
            bl[3 * h] = bl[3 * h] + total[:, :128]
            bl[3 * h + 1] = bl[3 * h + 1] + total[:, 128:]

    keep_near = jnp.where(c == 0, 1.0, 0.0).astype(F32)

    def direct(h, carry):
        for part in range(2):
            first_copy(h, part).wait_recv()
            relay_copy(h, part).start()
        o1, o2, slopes = block(d, h, 0, 384)
        res_ref[d, 0, :, head_cols(h)] = o1.astype(BF16)
        res_ref[d, 1, :, head_cols(h)] = o2.astype(BF16)
        framed = jnp.concatenate(
            [slopes[:, :128], slopes[:, 128:256] * keep_near, slopes[:, 256:], jnp.zeros((128, 128), F32)],
            axis=1,
        )
        diag = diagonals(framed, 512)
        back = pltpu.roll(diag, 511, 1)
        source = (1, 0, 3)
        for k in range(3):
            straight = diag[:, 128 * k : 128 * k + 128]
            turned = flip(back[:, 128 * source[k] : 128 * source[k] + 128])
            total = jnp.where(jnp.full((8, 128), c) == 0, straight, turned)
            bl[3 * h + k] = jnp.sum(total, axis=0, keepdims=True)

        @pl.when(h > 0)
        def _():
            other_near(h - 1)

        return carry

    me = x * n_grp + grp

    def rows_of(group, half):
        return pl.ds(9 * half, 9) if group == 0 else pl.ds(18 + 3 * half, 3)

    part_of = (pl.ds(0, 9), pl.ds(9, 3))

    def up_copy(group, half):
        return pltpu.make_async_remote_copy(
            src_ref=bl.at[rows_of(group, half)], dst_ref=r1.at[m, part_of[group]],
            send_sem=up_send, recv_sem=up_recv.at[group],
            device_id=line_peer(half), device_id_type=MESH,
        )

    def flat_copy(group, j):
        return pltpu.make_async_remote_copy(
            src_ref=r2.at[me, part_of[group]], dst_ref=r2.at[me, part_of[group]],
            send_sem=flat_send, recv_sem=flat_recv.at[group],
            device_id=plane_peer(j), device_id_type=MESH,
        )

    def down_copy(group, j):
        return pltpu.make_async_remote_copy(
            src_ref=fin.at[rows_of(group, c)], dst_ref=fin.at[rows_of(group, c)],
            send_sem=down_send, recv_sem=down_recv,
            device_id=line_peer(j), device_id_type=MESH,
        )

    def bytes_of(ref, send_sem, recv_sem):
        return pltpu.make_async_remote_copy(
            src_ref=ref, dst_ref=ref, send_sem=send_sem, recv_sem=recv_sem,
            device_id=sib, device_id_type=MESH,
        )

    def send_up(group):
        @pl.when(adds)
        def _():
            up_copy(group, 1 - c).start()
            r1[m, part_of[group]] = bl[rows_of(group, c)]

        @pl.when(jnp.logical_not(adds))
        def _():
            up_copy(group, 0).start()
            up_copy(group, 1).start()

    def add_line(group):
        part = part_of[group]
        others = r1.at[pl.ds(0, 23), part]
        bytes_of(others, up_send, up_recv.at[group]).wait_recv()
        r2[me, part] = jnp.sum(r1[:, part], axis=0)
        for j in range(1, 32):
            flat_copy(group, j).start()

    def add_plane(group):
        part = part_of[group]
        others = r2.at[pl.ds(0, 31), part]
        bytes_of(others, flat_send, flat_recv.at[group]).wait_recv()
        fin[rows_of(group, c)] = jnp.sum(r2[:, part], axis=0) * (n_seq * n_grp) ** (-0.5)
        down_copy(group, 1 - c).start()
        for j in range(2, 24):
            down_copy(group, j).start()

    lax.fori_loop(0, 7, direct, 0)
    send_up(0)
    direct(7, 0)
    other_near(7)
    send_up(1)

    def start_second(h, carry):
        for part in range(2):
            first_copy(h, part).wait_send()
            second_copy(h, part).start()
        return carry

    lax.fori_loop(0, H, start_second, 0)

    @pl.when(adds)
    def _():
        add_line(0)
        add_line(1)

    def finish(h, carry):
        for part in range(2):
            second_copy(h, part).wait_recv()
        o1, o2, _ = block(e, h, far_row(e), 128)
        res_ref[e, 0, :, head_cols(h)] = (acc[0, :, head_cols(h)] + o1).astype(BF16)
        res_ref[e, 1, :, head_cols(h)] = (acc[1, :, head_cols(h)] + o2).astype(BF16)
        return carry

    lax.fori_loop(0, H, finish, 0)
    for part in range(2):
        chip_copy(part).wait_send()

    def drain(h, carry):
        for part in range(2):
            relay_copy(h, part).wait_send()
            second_copy(h, part).wait_send()
        return carry

    lax.fori_loop(0, H, drain, 0)

    @pl.when(adds)
    def _():
        add_plane(0)
        add_plane(1)
        bytes_of(r1.at[0], up_send, down_recv).wait()
        bytes_of(r2.at[pl.ds(0, 31)], flat_send, down_recv).wait_send()
        bytes_of(r1.at[pl.ds(0, 23)], down_send, down_recv).wait_send()

    @pl.when(jnp.logical_not(adds))
    def _():
        bytes_of(fin, up_send, down_recv).wait()

    for h in range(H):
        for k in range(3):
            bg_ref[h : h + 1, 128 * k : 128 * k + 128] = fin[3 * h + k]


def copy_kernel(res_ref, bg_ref, att_ref, qg_ref, kg_ref, vg_ref, bias_ref, sem):
    copies = []
    for i, (side, part, ref) in enumerate(
        ((0, 0, att_ref), (0, 1, qg_ref), (1, 1, kg_ref), (1, 0, vg_ref))
    ):
        copy = pltpu.make_async_copy(res_ref.at[side, part], ref.at[0], sem.at[i])
        copy.start()
        copies.append(copy)
    copy = pltpu.make_async_copy(bg_ref, bias_ref, sem.at[4])
    copy.start()
    copies.append(copy)
    for copy in copies:
        copy.wait()


def on_device(queries, key_rows, value_rows, out_grad, positions, user_len, position_bias):
    hbm = pl.BlockSpec(memory_space=pltpu.HBM)
    vmem = pl.BlockSpec(memory_space=pltpu.VMEM)
    dma = pltpu.SemaphoreType.DMA
    res, bg = pl.pallas_call(
        main_kernel,
        out_shape=(
            jax.ShapeDtypeStruct((2, 2, BLOCK, D), BF16),
            jax.ShapeDtypeStruct((H, 384), F32),
        ),
        in_specs=[hbm] * 7,
        out_specs=(vmem, vmem),
        scratch_shapes=[
            pltpu.VMEM((2, 2, 384, D), BF16),
            pltpu.VMEM((2, H, 128, 384), F32),
            pltpu.VMEM((2, 128, 384), F32),
            pltpu.VMEM((H, 384), F32),
            pltpu.SMEM((2, 1), jnp.int32),
            pltpu.VMEM((2, 128, D), F32),
            pltpu.VMEM((24, 1, 128), F32),
            pltpu.VMEM((24, 12, 1, 128), F32),
            pltpu.VMEM((32, 12, 1, 128), F32),
            pltpu.VMEM((24, 1, 128), F32),
            dma((4,)),
            dma((2,)),
            dma((2,)),
            dma((H, 2)),
            dma((H, 2)),
            dma((H, 2)),
            dma((H, 2)),
            dma((H, 2)),
            dma((H, 2)),
            dma(()),
            dma((2,)),
            dma(()),
            dma((2,)),
            dma(()),
            dma(()),
            dma((3,)),
        ],
        compiler_params=pltpu.CompilerParams(
            collective_id=0, has_side_effects=True, vmem_limit_bytes=32 * 1024 * 1024
        ),
        name="attention",
    )(*(pltpu.with_memory_space_constraint(a, pltpu.HBM) for a in (queries, key_rows, value_rows, out_grad)), positions, user_len, pltpu.with_memory_space_constraint(position_bias, pltpu.HBM))
    whole = jax.ShapeDtypeStruct((1, BLOCK, D), BF16)
    return pl.pallas_call(
        copy_kernel,
        out_shape=(whole, whole, whole, whole, jax.ShapeDtypeStruct((H, 384), F32)),
        in_specs=[vmem, vmem],
        out_specs=(hbm,) * 5,
        scratch_shapes=[dma((5,))],
        compiler_params=pltpu.CompilerParams(vmem_limit_bytes=4 * 1024 * 1024),
        name="results",
    )(res, bg)


def solution(mesh):
    return jax.shard_map(
        on_device,
        mesh=mesh,
        in_specs=(
            P("grp", "seq", None),
            P("grp", "seq", None),
            P("grp", "seq", None),
            P("grp", "seq", None),
            P("grp", "seq"),
            P("grp", "seq"),
            P(),
        ),
        out_specs=(
            P("grp", "seq", None),
            P("grp", "seq", None),
            P("grp", "seq", None),
            P("grp", "seq", None),
            P(),
        ),
        check_vma=False,
    )
```

```python
import jax
import jax.numpy as jnp
from jax import lax
from jax.experimental import pallas as pl
from jax.experimental.pallas import tpu as pltpu
from jax.sharding import PartitionSpec as P

H = 8
BLOCK = 128
D = 1024
MESH = pl.DeviceIdType.MESH
F32 = jnp.float32
BF16 = jnp.bfloat16
SCALE = 128 ** -0.5


def own_row(side):
    return pl.multiple_of(256 * (1 - side), 128)


def far_row(side):
    return pl.multiple_of(256 * side, 128)


def head_cols(h):
    return pl.ds(pl.multiple_of(h * 128, 128), 128)


def flip(x):
    lane = lax.broadcasted_iota(jnp.int32, x.shape, 1)
    return jnp.take_along_axis(x, 127 - lane, axis=1, mode="promise_in_bounds")


def rolled(chunks, left):
    width = 128 - left
    lane = lax.broadcasted_iota(jnp.int32, (8, 128), 1)
    turned = [pltpu.roll(chunk, width, 1) for chunk in chunks]
    return [
        jnp.where(lane < width, turned[k], turned[(k + 1) % len(chunks)])
        for k in range(len(chunks))
    ]


def nt(a, b):
    return lax.dot_general(a, b, (((1,), (1,)), ((), ())), preferred_element_type=F32)


def diagonals(slopes, width, extra):
    count = width // 128
    slabs = []
    for i in range(16):
        chunks = [slopes[8 * i : 8 * i + 8, 128 * k : 128 * k + 128] for k in range(count)]
        slabs.append(rolled(chunks + [jnp.zeros((8, 128), F32)], 8 * i + extra))
    while len(slabs) > 1:
        slabs = [
            [a + b for a, b in zip(slabs[k], slabs[k + 1])] for k in range(0, len(slabs), 2)
        ]
    chunks = slabs[0]
    row = lax.broadcasted_iota(jnp.int32, (8, 128), 0)
    for bit in (1, 2, 4):
        moved = rolled(chunks, bit)
        chunks = [jnp.where((row & bit) != 0, b, a) for a, b in zip(chunks, moved)]
    return chunks


def row_sum(x):
    return jnp.sum(x, axis=0, keepdims=True)


def main_kernel(
    q_ref, k_ref, v_ref, g_ref, pos_ref, len_ref, bias_ref,
    res_ref, bg_ref,
    wide, sibling, sibling_mask, toep, mask, bias, place, wts, slp, bl, r1, r2, fin,
    load_sem, chip_send, chip_recv, extra_send, extra_recv, w1_send, w1_recv, rel_send, rel_recv, w2_send, w2_recv,
    up_send, up_recv, flat_send, flat_recv, down_send, down_recv, small_sem,
):
    s = lax.axis_index("seq")
    grp = lax.axis_index("grp")
    n_seq = lax.axis_size("seq")
    n_grp = lax.axis_size("grp")
    c = s % 2
    x = s // 24
    m = s % 24
    d = 1 - c
    e = c
    sib = {"seq": s + 1 - 2 * c, "grp": grp}
    ahead = {"seq": (s + 4 * c - 2 + n_seq) % n_seq, "grp": grp}
    behind = {"seq": (s + 2 - 4 * c + n_seq) % n_seq, "grp": grp}

    loads = []
    for i, (ref, side, part) in enumerate(
        ((q_ref, 1, 0), (g_ref, 1, 1), (k_ref, 0, 0), (v_ref, 0, 1))
    ):
        row = 256 * (1 - side)
        copy = pltpu.make_async_copy(
            ref.at[0], wide.at[side, part, pl.ds(row, 128)], load_sem.at[i]
        )
        copy.start()
        loads.append(copy)

    smalls = []
    for i, (src, dst) in enumerate(
        ((bias_ref, bias), (pos_ref, place.at[pl.ds(0, 1)]), (len_ref, place.at[pl.ds(1, 1)]))
    ):
        copy = pltpu.make_async_copy(src, dst, small_sem.at[i])
        copy.start()
        smalls.append(copy)
    barrier = pltpu.get_barrier_semaphore()

    def greet(device):
        pl.semaphore_signal(barrier, inc=1, device_id=device, device_id_type=MESH)

    def line_peer(j):
        return {"seq": s - m + j, "grp": grp}

    def plane_peer(j):
        t = (x * n_grp + grp + j) % 32
        return {"seq": (t // n_grp) * 24 + m, "grp": t % n_grp}

    adds = m < 2
    greet(ahead)
    greet(behind)
    greet(sib)

    @pl.when(adds)
    def _():
        for j in range(1, 32):
            greet(plane_peer(j))
        for j in range(2, 24):
            greet(line_peer(j))

    for copy in loads:
        copy.wait()

    @pl.when(adds)
    def _():
        pl.semaphore_wait(barrier, 3 + 31)

    @pl.when(jnp.logical_not(adds))
    def _():
        pl.semaphore_wait(barrier, 3 + 2)

    def piece(side, part, rows, h):
        return wide.at[side, part, pl.ds(rows, 128), head_cols(h)]

    def first_copy(h, part):
        return pltpu.make_async_remote_copy(
            src_ref=piece(d, part, own_row(d), h), dst_ref=piece(d, part, far_row(d), h),
            send_sem=w1_send.at[h, part], recv_sem=w1_recv.at[h, part],
            device_id=ahead, device_id_type=MESH,
        )

    def second_copy(h, part):
        return pltpu.make_async_remote_copy(
            src_ref=piece(e, part, own_row(e), h), dst_ref=piece(e, part, far_row(e), h),
            send_sem=w2_send.at[h, part], recv_sem=w2_recv.at[h, part],
            device_id=behind, device_id_type=MESH,
        )

    def relay_copy(h, part):
        return pltpu.make_async_remote_copy(
            src_ref=piece(d, part, far_row(d), h), dst_ref=piece(d, part, 128, h),
            send_sem=rel_send.at[h, part], recv_sem=rel_recv.at[h, part],
            device_id=sib, device_id_type=MESH,
        )

    def chip_copy(part):
        return pltpu.make_async_remote_copy(
            src_ref=wide.at[e, part, pl.ds(own_row(e), 128)],
            dst_ref=wide.at[e, part, pl.ds(128, 128)],
            send_sem=chip_send.at[part], recv_sem=chip_recv.at[part],
            device_id=sib, device_id_type=MESH,
        )

    for h in range(H):
        first_copy(h, 0).start()
        first_copy(h, 1).start()
    chip_copy(0).start()
    chip_copy(1).start()

    def extra_copy(part):
        return pltpu.make_async_remote_copy(
            src_ref=wide.at[0, part, pl.ds(256, 128)], dst_ref=sibling.at[part],
            send_sem=extra_send.at[part], recv_sem=extra_recv.at[part],
            device_id=sib, device_id_type=MESH,
        )

    def extra_mask():
        return pltpu.make_async_remote_copy(
            src_ref=mask.at[1, pl.ds(0, 8), pl.ds(128, 128)], dst_ref=sibling_mask,
            send_sem=extra_send.at[2], recv_sem=extra_recv.at[2],
            device_id=sib, device_id_type=MESH,
        )

    @pl.when(c == 1)
    def _():
        extra_copy(0).start()
        extra_copy(1).start()

    for copy in smalls:
        copy.wait()
    p = place[0, 0]
    n = place[1, 0]
    row = lax.broadcasted_iota(jnp.int32, (128, 384), 0)
    lane = lax.broadcasted_iota(jnp.int32, (128, 384), 1)
    inverse = 1.0 / jnp.full((128, 384), n, jnp.int32).astype(F32)
    used = (row < n - p * 128) & (lane >= 256 - 128 * p) & (lane <= 256 + row)
    mask[0] = jnp.where(used, inverse, 0.0)
    used = (lane < n - p * 128) & (lane >= row)
    mask[1] = jnp.where(used, inverse, 0.0)

    def make_toep(side):
        def body(h, carry):
            b = jnp.broadcast_to(bias[pl.ds(h, 1), :] * 0.5, (8, 384))
            b0, b1, b2 = b[:, :128], b[:, 128:256], b[:, 256:]
            zero = jnp.zeros_like(b0)
            keyed = jnp.concatenate([b0, b1, b2, zero], axis=1)
            back = jnp.concatenate([flip(b1), flip(b0), zero, flip(b2)], axis=1)
            base = jnp.where(side == 1, keyed, pltpu.roll(back, 1, 1))
            base = jnp.broadcast_to(base[0:1], (128, 512))
            toep[side, h] = pltpu.roll(base, 0, 1, stride=1, stride_axis=0)[:, :384]
            return carry

        lax.fori_loop(0, H, body, 0, unroll=2)

    @pl.when(c == 1)
    def _():
        extra_mask().start()

    make_toep(d)
    make_toep(e)

    def scores(side, h, lo, width):
        cols = head_cols(h)
        rows = pl.ds(lo, width)
        other = 1 - side
        own = pl.ds(own_row(other), 128)
        y = nt(wide[other, 0, own, cols], wide[side, 0, rows, cols])
        y = y * (0.5 * SCALE) + toep[side, h, :, rows]
        pulled = nt(wide[other, 1, own, cols], wide[side, 1, rows, cols])
        t = jnp.tanh(y)
        w0 = y * t + y
        sg = 0.5 * t + 0.5
        mk = mask[side, :, rows]
        slopes = pulled * (sg + w0 * (1.0 - sg)) * mk
        wts[side, h, :, rows] = (w0 * mk).astype(BF16)
        slp[side, h, :, rows] = slopes.astype(BF16)
        return slopes

    def outputs(side, h):
        cols = head_cols(h)
        o1 = jnp.dot(wts[side, h], wide[side, 1, :, cols], preferred_element_type=F32)
        o2 = jnp.dot(slp[side, h], wide[side, 0, :, cols], preferred_element_type=F32)
        res_ref[side, 0, :, cols] = o1.astype(BF16)
        res_ref[side, 1, :, cols] = (o2 * SCALE).astype(BF16)

    def near_row(side):
        return pl.multiple_of(128 * (1 - side), 128)

    first_core = c == 0

    def direct_near(h):
        slopes = scores(d, h, near_row(d), 256)
        lanes = lax.broadcasted_iota(jnp.int32, (128, 256), 1)
        slopes = jnp.where(first_core | (lanes >= 128), slopes, 0.0)
        n0, n1, _ = diagonals(slopes, 256, c)
        bl[3 * h] = row_sum(jnp.where(first_core, n0, flip(n0)))
        bl[3 * h + 1] = row_sum(n1)

    def first_far(h):
        cols = head_cols(h)
        f0, f1 = diagonals(scores(1, h, 256, 128), 128, 0)
        y = nt(sibling[0, :, cols], wide[1, 0, 256:, cols]) * (0.5 * SCALE) + toep[1, h, :, 128:256]
        pulled = nt(sibling[1, :, cols], wide[1, 1, 256:, cols])
        t = jnp.tanh(y)
        w0 = y * t + y
        sg = 0.5 * t + 0.5
        slopes = pulled * (sg + w0 * (1.0 - sg)) * sibling_mask[0:1, :]
        g0, g1 = diagonals(slopes, 128, 0)
        bl[3 * h] = bl[3 * h] + row_sum(g1)
        bl[3 * h + 1] = bl[3 * h + 1] + row_sum(f1 + g0)
        bl[3 * h + 2] = row_sum(f0)

    def second_far(h):
        f0, f1 = diagonals(scores(0, h, 0, 128), 128, 1)
        bl[3 * h + 1] = row_sum(flip(f0))
        bl[3 * h + 2] = row_sum(flip(f1))

    chip_copy(0).wait_recv()
    chip_copy(1).wait_recv()

    def start_near(i, carry):
        for h in range(4):
            direct_near(4 * i + h)
        return carry

    lax.fori_loop(0, 2, start_near, 0)

    @pl.when(c == 0)
    def _():
        for part in range(2):
            extra_copy(part).wait_recv()
        extra_mask().wait_recv()

    def arrive(group):
        heads = (2 * group, 2 * group + 1)
        for h in heads:
            for part in range(2):
                first_copy(h, part).wait_recv()
                relay_copy(h, part).start()

        @pl.when(c == 0)
        def _():
            for h in heads:
                first_far(h)

        @pl.when(c == 1)
        def _():
            for h in heads:
                second_far(h)

    me = x * n_grp + grp
    order = [8 * i + j for j in (0, 1, 2, 3, 7, 6, 4, 5) for i in (0, 2, 3, 1)]

    def rows_of(group, half):
        return pl.ds(6 * half, 6) if group == 0 else pl.ds(6 + 6 * group + 3 * half, 3)

    part_of = (pl.ds(0, 6), pl.ds(6, 3), pl.ds(9, 3))

    def up_copy(group, half):
        return pltpu.make_async_remote_copy(
            src_ref=bl.at[rows_of(group, half)], dst_ref=r1.at[m, part_of[group]],
            send_sem=up_send, recv_sem=up_recv.at[group],
            device_id=line_peer(half), device_id_type=MESH,
        )

    def flat_copy(group, j):
        return pltpu.make_async_remote_copy(
            src_ref=r2.at[me, part_of[group]], dst_ref=r2.at[me, part_of[group]],
            send_sem=flat_send, recv_sem=flat_recv.at[group],
            device_id={"seq": (j // 8) * 24 + m, "grp": j % 8}, device_id_type=MESH,
        )

    def down_copy(group, j):
        return pltpu.make_async_remote_copy(
            src_ref=fin.at[rows_of(group, c)], dst_ref=fin.at[rows_of(group, c)],
            send_sem=down_send, recv_sem=down_recv,
            device_id=line_peer(j), device_id_type=MESH,
        )

    def bytes_of(ref, send_sem, recv_sem):
        return pltpu.make_async_remote_copy(
            src_ref=ref, dst_ref=ref, send_sem=send_sem, recv_sem=recv_sem,
            device_id=sib, device_id_type=MESH,
        )

    def send_up(group):
        @pl.when(adds)
        def _():
            up_copy(group, 1 - c).start()
            r1[m, part_of[group]] = bl[rows_of(group, c)]

        @pl.when(jnp.logical_not(adds))
        def _():
            up_copy(group, 0).start()
            up_copy(group, 1).start()

    def add_line(group):
        part = part_of[group]
        others = r1.at[pl.ds(0, 23), part]
        bytes_of(others, up_send, up_recv.at[group]).wait_recv()
        r2[me, part] = jnp.sum(r1[:, part], axis=0)
        for j in order:

            @pl.when(me != j)
            def _(j=j):
                flat_copy(group, j).start()

    def add_plane(group):
        part = part_of[group]
        others = r2.at[pl.ds(0, 31), part]
        bytes_of(others, flat_send, flat_recv.at[group]).wait_recv()
        fin[rows_of(group, c)] = jnp.sum(r2[:, part], axis=0) * (n_seq * n_grp) ** (-0.5)
        down_copy(group, 1 - c).start()
        for j in range(2, 24):
            down_copy(group, j).start()

    arrive(0)
    arrive(1)
    send_up(0)
    arrive(2)
    send_up(1)
    arrive(3)
    send_up(2)

    def start_second(h, carry):
        for part in range(2):
            first_copy(h, part).wait_send()
            second_copy(h, part).start()
        return carry

    lax.fori_loop(0, H, start_second, 0)

    def rest(i, carry):
        for h in range(2):
            outputs(d, 2 * i + h)
            for part in range(2):
                relay_copy(2 * i + h, part).wait_recv()
            scores(e, 2 * i + h, near_row(e), 256)
        return carry

    lax.fori_loop(0, H // 2, rest, 0)

    @pl.when(adds)
    def _():
        for group in range(3):
            add_line(group)

    def finish(i, carry):
        for h in range(2):
            for part in range(2):
                second_copy(2 * i + h, part).wait_recv()
        for h in range(2):
            scores(e, 2 * i + h, far_row(e), 128)
        for h in range(2):
            outputs(e, 2 * i + h)
        return carry

    lax.fori_loop(0, H // 2, finish, 0)
    for part in range(2):
        chip_copy(part).wait_send()

    @pl.when(c == 1)
    def _():
        for part in range(2):
            extra_copy(part).wait_send()
        extra_mask().wait_send()

    def drain(h, carry):
        for part in range(2):
            relay_copy(h, part).wait_send()
            second_copy(h, part).wait_send()
        return carry

    lax.fori_loop(0, H, drain, 0)

    @pl.when(adds)
    def _():
        for group in range(3):
            add_plane(group)
        bytes_of(r1.at[0], up_send, down_recv).wait()
        bytes_of(r2.at[pl.ds(0, 31)], flat_send, down_recv).wait_send()
        bytes_of(r1.at[pl.ds(0, 23)], down_send, down_recv).wait_send()

    @pl.when(jnp.logical_not(adds))
    def _():
        bytes_of(fin, up_send, down_recv).wait()

    for h in range(H):
        for k in range(3):
            bg_ref[h : h + 1, 128 * k : 128 * k + 128] = fin[3 * h + k]


def copy_kernel(res_ref, bg_ref, att_ref, qg_ref, kg_ref, vg_ref, bias_ref, sem):
    copies = []
    for i, (side, part, ref) in enumerate(
        ((0, 0, att_ref), (0, 1, qg_ref), (1, 1, kg_ref), (1, 0, vg_ref))
    ):
        copy = pltpu.make_async_copy(res_ref.at[side, part], ref.at[0], sem.at[i])
        copy.start()
        copies.append(copy)
    copy = pltpu.make_async_copy(bg_ref, bias_ref, sem.at[4])
    copy.start()
    copies.append(copy)
    for copy in copies:
        copy.wait()


def on_device(queries, key_rows, value_rows, out_grad, positions, user_len, position_bias):
    hbm = pl.BlockSpec(memory_space=pltpu.HBM)
    vmem = pl.BlockSpec(memory_space=pltpu.VMEM)
    dma = pltpu.SemaphoreType.DMA
    res, bg = pl.pallas_call(
        main_kernel,
        out_shape=(
            jax.ShapeDtypeStruct((2, 2, BLOCK, D), BF16),
            jax.ShapeDtypeStruct((H, 384), F32),
        ),
        in_specs=[hbm] * 7,
        out_specs=(vmem, vmem),
        scratch_shapes=[
            pltpu.VMEM((2, 2, 384, D), BF16),
            pltpu.VMEM((2, 128, D), BF16),
            pltpu.VMEM((8, 128), F32),
            pltpu.VMEM((2, H, 128, 384), F32),
            pltpu.VMEM((2, 128, 384), F32),
            pltpu.VMEM((H, 384), F32),
            pltpu.SMEM((2, 1), jnp.int32),
            pltpu.VMEM((2, H, 128, 384), BF16),
            pltpu.VMEM((2, H, 128, 384), BF16),
            pltpu.VMEM((24, 1, 128), F32),
            pltpu.VMEM((24, 12, 1, 128), F32),
            pltpu.VMEM((32, 12, 1, 128), F32),
            pltpu.VMEM((24, 1, 128), F32),
            dma((4,)),
            dma((2,)),
            dma((2,)),
            dma((3,)),
            dma((3,)),
            dma((H, 2)),
            dma((H, 2)),
            dma((H, 2)),
            dma((H, 2)),
            dma((H, 2)),
            dma((H, 2)),
            dma(()),
            dma((3,)),
            dma(()),
            dma((3,)),
            dma(()),
            dma(()),
            dma((3,)),
        ],
        compiler_params=pltpu.CompilerParams(
            collective_id=0, has_side_effects=True, vmem_limit_bytes=32 * 1024 * 1024
        ),
        name="attention",
    )(*(pltpu.with_memory_space_constraint(a, pltpu.HBM) for a in (queries, key_rows, value_rows, out_grad)), positions, user_len, pltpu.with_memory_space_constraint(position_bias, pltpu.HBM))
    whole = jax.ShapeDtypeStruct((1, BLOCK, D), BF16)
    return pl.pallas_call(
        copy_kernel,
        out_shape=(whole, whole, whole, whole, jax.ShapeDtypeStruct((H, 384), F32)),
        in_specs=[vmem, vmem],
        out_specs=(hbm,) * 5,
        scratch_shapes=[dma((5,))],
        compiler_params=pltpu.CompilerParams(vmem_limit_bytes=4 * 1024 * 1024),
        name="results",
    )(res, bg)


def solution(mesh):
    return jax.shard_map(
        on_device,
        mesh=mesh,
        in_specs=(
            P("grp", "seq", None),
            P("grp", "seq", None),
            P("grp", "seq", None),
            P("grp", "seq", None),
            P("grp", "seq"),
            P("grp", "seq"),
            P(),
        ),
        out_specs=(
            P("grp", "seq", None),
            P("grp", "seq", None),
            P("grp", "seq", None),
            P("grp", "seq", None),
            P(),
        ),
        check_vma=False,
    )
```

```python
import jax
import jax.numpy as jnp
from jax import lax
from jax.experimental import pallas as pl
from jax.experimental.pallas import tpu as pltpu
from jax.sharding import PartitionSpec as P

H = 8
BLOCK = 128
D = 1024
MESH = pl.DeviceIdType.MESH
F32 = jnp.float32
BF16 = jnp.bfloat16
SCALE = 128 ** -0.5


def own_row(side):
    return pl.multiple_of(256 * (1 - side), 128)


def far_row(side):
    return pl.multiple_of(256 * side, 128)


def head_cols(h):
    return pl.ds(pl.multiple_of(h * 128, 128), 128)


def flip(x):
    lane = lax.broadcasted_iota(jnp.int32, x.shape, 1)
    return jnp.take_along_axis(x, 127 - lane, axis=1, mode="promise_in_bounds")


def rolled(chunks, left):
    width = 128 - left
    lane = lax.broadcasted_iota(jnp.int32, (8, 128), 1)
    turned = [pltpu.roll(chunk, width, 1) for chunk in chunks]
    return [
        jnp.where(lane < width, turned[k], turned[(k + 1) % len(chunks)])
        for k in range(len(chunks))
    ]


def nt(a, b):
    return lax.dot_general(a, b, (((1,), (1,)), ((), ())), preferred_element_type=F32)


def diagonals(slopes, width, extra):
    count = width // 128
    slabs = []
    for i in range(16):
        chunks = [slopes[8 * i : 8 * i + 8, 128 * k : 128 * k + 128] for k in range(count)]
        slabs.append(rolled(chunks + [jnp.zeros((8, 128), F32)], 8 * i + extra))
    while len(slabs) > 1:
        slabs = [
            [a + b for a, b in zip(slabs[k], slabs[k + 1])] for k in range(0, len(slabs), 2)
        ]
    chunks = slabs[0]
    row = lax.broadcasted_iota(jnp.int32, (8, 128), 0)
    for bit in (1, 2, 4):
        moved = rolled(chunks, bit)
        chunks = [jnp.where((row & bit) != 0, b, a) for a, b in zip(chunks, moved)]
    return chunks


def row_sum(x):
    return jnp.sum(x, axis=0, keepdims=True)


def main_kernel(
    q_ref, k_ref, v_ref, g_ref, pos_ref, len_ref, bias_ref,
    res_ref, bg_ref,
    wide, sibling, sibling_mask, mixed_out, mixed_in, toep, mask, bias, place, wts, slp, bl, r1, r2, fin,
    load_sem, chip_send, chip_recv, extra_send, extra_recv, mask_send, mask_recv, mix_send, mix_recv, w1_send, w1_recv, rel_send, rel_recv, w2_send, w2_recv,
    up_send, up_recv, flat_send, flat_recv, down_send, down_recv, small_sem,
):
    s = lax.axis_index("seq")
    grp = lax.axis_index("grp")
    n_seq = lax.axis_size("seq")
    n_grp = lax.axis_size("grp")
    c = s % 2
    x = s // 24
    m = s % 24
    d = 1 - c
    e = c
    sib = {"seq": s + 1 - 2 * c, "grp": grp}
    ahead = {"seq": (s + 4 * c - 2 + n_seq) % n_seq, "grp": grp}
    behind = {"seq": (s + 2 - 4 * c + n_seq) % n_seq, "grp": grp}

    barrier = pltpu.get_barrier_semaphore()

    def greet(device):
        pl.semaphore_signal(barrier, inc=1, device_id=device, device_id_type=MESH)

    def line_peer(j):
        return {"seq": s - m + j, "grp": grp}

    def plane_peer(j):
        t = (x * n_grp + grp + j) % 32
        return {"seq": (t // n_grp) * 24 + m, "grp": t % n_grp}

    adds = m < 2
    greet(ahead)
    greet(behind)
    greet(sib)

    loads = []
    for i, (ref, side, part) in enumerate(
        ((q_ref, 1, 0), (g_ref, 1, 1), (k_ref, 0, 0), (v_ref, 0, 1))
    ):
        row = 256 * (1 - side)
        copy = pltpu.make_async_copy(
            ref.at[0], wide.at[side, part, pl.ds(row, 128)], load_sem.at[i]
        )
        copy.start()
        loads.append(copy)

    smalls = []
    for i, (src, dst) in enumerate(
        ((bias_ref, bias), (pos_ref, place.at[pl.ds(0, 1)]), (len_ref, place.at[pl.ds(1, 1)]))
    ):
        copy = pltpu.make_async_copy(src, dst, small_sem.at[i])
        copy.start()
        smalls.append(copy)
    @pl.when(adds)
    def _():
        for j in range(1, 32):
            greet(plane_peer(j))
        for j in range(2, 24):
            greet(line_peer(j))

    for copy in loads:
        copy.wait()

    @pl.when(adds)
    def _():
        pl.semaphore_wait(barrier, 3 + 31)

    @pl.when(jnp.logical_not(adds))
    def _():
        pl.semaphore_wait(barrier, 3 + 2)

    def piece(side, part, rows, h):
        return wide.at[side, part, pl.ds(rows, 128), head_cols(h)]

    def first_copy(h, part):
        return pltpu.make_async_remote_copy(
            src_ref=piece(d, part, own_row(d), h), dst_ref=piece(d, part, far_row(d), h),
            send_sem=w1_send.at[h, part], recv_sem=w1_recv.at[h, part],
            device_id=ahead, device_id_type=MESH,
        )

    def second_copy(h, part):
        return pltpu.make_async_remote_copy(
            src_ref=piece(e, part, own_row(e), h), dst_ref=piece(e, part, far_row(e), h),
            send_sem=w2_send.at[h, part], recv_sem=w2_recv.at[h, part],
            device_id=behind, device_id_type=MESH,
        )

    def relay_copy(h, part):
        return pltpu.make_async_remote_copy(
            src_ref=piece(d, part, far_row(d), h), dst_ref=piece(d, part, 128, h),
            send_sem=rel_send.at[h, part], recv_sem=rel_recv.at[h, part],
            device_id=sib, device_id_type=MESH,
        )

    def chip_copy(part, rest):
        cols = pl.ds(pl.multiple_of(256 * (1 - c), 128), 768) if rest else pl.ds(pl.multiple_of(768 * c, 128), 256)
        return pltpu.make_async_remote_copy(
            src_ref=wide.at[e, part, pl.ds(own_row(e), 128), cols],
            dst_ref=wide.at[e, part, pl.ds(128, 128), cols],
            send_sem=chip_send.at[part, rest], recv_sem=chip_recv.at[part, rest],
            device_id=sib, device_id_type=MESH,
        )

    def extra_copy(part):
        return pltpu.make_async_remote_copy(
            src_ref=wide.at[d, part, pl.ds(own_row(d), 128)], dst_ref=sibling.at[part],
            send_sem=extra_send.at[part], recv_sem=extra_recv.at[part],
            device_id=sib, device_id_type=MESH,
        )

    def mixed_copy(part):
        return pltpu.make_async_remote_copy(
            src_ref=mixed_out.at[part], dst_ref=mixed_in.at[part],
            send_sem=mix_send.at[part], recv_sem=mix_recv.at[part],
            device_id=ahead, device_id_type=MESH,
        )

    def mask_copy(core):
        if core == 0:
            src, dst = mask.at[0, :, pl.ds(0, 256)], sibling_mask
        else:
            src, dst = mask.at[1, pl.ds(0, 8), pl.ds(128, 256)], sibling_mask.at[pl.ds(0, 8)]
        return pltpu.make_async_remote_copy(
            src_ref=src, dst_ref=dst, send_sem=mask_send, recv_sem=mask_recv,
            device_id=sib, device_id_type=MESH,
        )

    lead = 6 - 6 * c
    lack = 6 * c
    for part in range(2):
        chip_copy(part, 0).start()
    for h in (lead, lead + 1):
        first_copy(h, 0).start()
        first_copy(h, 1).start()
    for part in range(2):
        chip_copy(part, 1).start()
    for part in range(2):
        extra_copy(part).start()

    for copy in smalls:
        copy.wait()
    p = place[0, 0]
    n = place[1, 0]
    row = lax.broadcasted_iota(jnp.int32, (128, 384), 0)
    lane = lax.broadcasted_iota(jnp.int32, (128, 384), 1)
    inverse = 1.0 / jnp.full((128, 384), n, jnp.int32).astype(F32)
    used = (row < n - p * 128) & (lane >= 256 - 128 * p) & (lane <= 256 + row)
    mask[0] = jnp.where(used, inverse, 0.0)
    used = (lane < n - p * 128) & (lane >= row)
    mask[1] = jnp.where(used, inverse, 0.0)

    for part in range(2):
        chip_copy(part, 0).wait_recv()
    use_sibling = jnp.where(p == 1, 1, 0) * jnp.where(n > 256, 1, 0)
    for part in range(2):
        theirs = wide[d, part, pl.ds(128, 128), pl.ds(pl.multiple_of(128 * lead, 128), 256)]
        mine = wide[d, part, pl.ds(own_row(d), 128), pl.ds(256, 256)]
        mixed_out[part] = jnp.where(use_sibling == 1, theirs, mine)
        mixed_copy(part).start()
    for h in (4, 5):
        first_copy(h, 0).start()
        first_copy(h, 1).start()

    @pl.when(c == 0)
    def _():
        mask_copy(0).start()

    @pl.when(c == 1)
    def _():
        mask_copy(1).start()

    def make_toep(side):
        def body(h, carry):
            b = jnp.broadcast_to(bias[pl.ds(h, 1), :] * 0.5, (8, 384))
            b0, b1, b2 = b[:, :128], b[:, 128:256], b[:, 256:]
            zero = jnp.zeros_like(b0)
            keyed = jnp.concatenate([b0, b1, b2, zero], axis=1)
            back = jnp.concatenate([flip(b1), flip(b0), zero, flip(b2)], axis=1)
            base = jnp.where(side == 1, keyed, pltpu.roll(back, 1, 1))
            base = jnp.broadcast_to(base[0:1], (128, 512))
            toep[side, h] = pltpu.roll(base, 0, 1, stride=1, stride_axis=0)[:, :384]
            return carry

        lax.fori_loop(0, H, body, 0, unroll=2)


    make_toep(d)
    make_toep(e)

    def entries(x, y, x3, y3, near, mk):
        z = nt(x, x3) * (0.5 * SCALE) + near
        pulled = nt(y, y3)
        t = jnp.tanh(z)
        w0 = z * t + z
        sg = 0.5 * t + 0.5
        return w0 * mk, pulled * (sg + w0 * (1.0 - sg)) * mk

    def scores(side, h, lo, width, moved=None):
        cols = head_cols(h)
        rows = pl.ds(lo, width)
        other = 1 - side
        own = pl.ds(own_row(other), 128)
        x3, y3 = (wide[side, 0, rows, cols], wide[side, 1, rows, cols]) if moved is None else moved
        weights, slopes = entries(
            wide[other, 0, own, cols], wide[other, 1, own, cols], x3, y3,
            toep[side, h, :, rows], mask[side, :, rows],
        )
        wts[side, h, :, rows] = weights.astype(BF16)
        slp[side, h, :, rows] = slopes.astype(BF16)
        return slopes

    def sibling_scores(side, h, lo, x3, y3, mk):
        cols = head_cols(h)
        return entries(sibling[0, :, cols], sibling[1, :, cols], x3, y3, toep[side, h, :, lo : lo + 128], mk)[1]

    def outputs(side, h):
        cols = head_cols(h)
        o1 = jnp.dot(wts[side, h], wide[side, 1, :, cols], preferred_element_type=F32)
        o2 = jnp.dot(slp[side, h], wide[side, 0, :, cols], preferred_element_type=F32)
        res_ref[side, 0, :, cols] = o1.astype(BF16)
        res_ref[side, 1, :, cols] = (o2 * SCALE).astype(BF16)

    first_core = c == 0
    at = (0, 3, 6, 9, 18, 21, 12, 15)

    def count(h, offset, slopes, turned):
        f0, f1 = diagonals(slopes, 128, 1 if turned else 0)
        low, high = (flip(f0), flip(f1)) if turned else (f1, f0)
        k = at[h] + offset - 1
        bl[k] = bl[k] + row_sum(low)
        bl[k + 1] = bl[k + 1] + row_sum(high)

    for part in range(2):
        chip_copy(part, 1).wait_recv()

    def direct_near(h):
        slopes = scores(d, h, pl.multiple_of(128 * (1 - d), 128), 256)
        lanes = lax.broadcasted_iota(jnp.int32, (128, 256), 1)
        slopes = jnp.where(first_core | (lanes >= 128), slopes, 0.0)
        n0, n1, _ = diagonals(slopes, 256, c)
        bl[at[h]] = row_sum(jnp.where(first_core, n0, flip(n0)))
        bl[at[h] + 1] = row_sum(jnp.where(first_core, n1, 0.0))
        bl[at[h] + 2] = jnp.zeros((1, 128), F32)

    for h in range(H):
        direct_near(h)

    for part in range(2):
        extra_copy(part).wait_recv()

    @pl.when(c == 0)
    def _():
        mask_copy(1).wait_recv()

    @pl.when(c == 1)
    def _():
        mask_copy(0).wait_recv()

    def relay(h):
        for part in range(2):
            first_copy(h, part).wait_recv()
            relay_copy(h, part).start()

    def far_pairs(h, turned, siblings):
        cols = head_cols(h)
        if turned:
            count(h, 2, scores(0, h, 0, 128), True)
            if siblings:
                mk = sibling_mask[:, 128:]
                count(h, 1, sibling_scores(0, h, 128, wide[0, 0, :128, cols], wide[0, 1, :128, cols], mk), True)
        else:
            count(h, 2, scores(1, h, 256, 128), False)
            mk = sibling_mask[0:1, :128]
            count(h, 1, sibling_scores(1, h, 128, wide[1, 0, 256:, cols], wide[1, 1, 256:, cols], mk), False)

    def mixed_pairs(turned):
        for i in range(2):
            moved = tuple(mixed_in[part, :, 128 * i : 128 * i + 128] for part in range(2))
            if turned:
                count(2 + i, 2, scores(0, 2 + i, 0, 128, moved), True)
                third = sibling_mask[:, :128]
                count(i, 2, sibling_scores(0, i, 0, *moved, third), True)
                second = jnp.where(third > 0.0, 0.0, sibling_mask[:, 128:])
                count(2 + i, 1, sibling_scores(0, 2 + i, 128, *moved, second), True)
            else:
                count(2 + i, 2, scores(1, 2 + i, 256, 128, moved), False)
                second = jnp.where(mask[1, 0:1, 256:] > 0.0, sibling_mask[0:1, :128], 0.0)
                count(2 + i, 1, sibling_scores(1, 2 + i, 128, *moved, second), False)
                third = sibling_mask[0:1, 128:]
                count(6 + i, 2, sibling_scores(1, 6 + i, 256, *moved, third), False)

    def both(todo):
        @pl.when(c == 0)
        def _():
            todo(False)

        @pl.when(c == 1)
        def _():
            todo(True)

    def arrive_lead(turned):
        for h in (0, 1) if turned else (6, 7):
            relay(h)
        for h in (0, 1) if turned else (6, 7):
            far_pairs(h, turned, True)

    def arrive_one(h):
        relay(h)
        both(lambda turned: far_pairs(h, turned, False))

    def arrive_mixed():
        for part in range(2):
            mixed_copy(part).wait_recv()
        both(mixed_pairs)

    me = x * n_grp + grp
    order = [8 * i + j for j in (0, 1, 2, 3, 7, 6, 4, 5) for i in (0, 2, 3, 1)]

    def rows_of(group, half):
        return pl.ds(9 * half, 9) if group == 0 else pl.ds(18 + 3 * half, 3)

    part_of = (pl.ds(0, 9), pl.ds(9, 3))

    def up_copy(group, half):
        return pltpu.make_async_remote_copy(
            src_ref=bl.at[rows_of(group, half)], dst_ref=r1.at[m, part_of[group]],
            send_sem=up_send, recv_sem=up_recv.at[group],
            device_id=line_peer(half), device_id_type=MESH,
        )

    def flat_copy(group, j):
        return pltpu.make_async_remote_copy(
            src_ref=r2.at[me, part_of[group]], dst_ref=r2.at[me, part_of[group]],
            send_sem=flat_send, recv_sem=flat_recv.at[group],
            device_id={"seq": (j // 8) * 24 + m, "grp": j % 8}, device_id_type=MESH,
        )

    def down_copy(group, j):
        return pltpu.make_async_remote_copy(
            src_ref=fin.at[rows_of(group, c)], dst_ref=fin.at[rows_of(group, c)],
            send_sem=down_send, recv_sem=down_recv,
            device_id=line_peer(j), device_id_type=MESH,
        )

    def bytes_of(ref, send_sem, recv_sem):
        return pltpu.make_async_remote_copy(
            src_ref=ref, dst_ref=ref, send_sem=send_sem, recv_sem=recv_sem,
            device_id=sib, device_id_type=MESH,
        )

    def send_up(group):
        @pl.when(adds)
        def _():
            up_copy(group, 1 - c).start()
            r1[m, part_of[group]] = bl[rows_of(group, c)]

        @pl.when(jnp.logical_not(adds))
        def _():
            up_copy(group, 0).start()
            up_copy(group, 1).start()

    def add_line(group):
        part = part_of[group]
        others = r1.at[pl.ds(0, 23), part]
        bytes_of(others, up_send, up_recv.at[group]).wait_recv()
        r2[me, part] = jnp.sum(r1[:, part], axis=0)
        for j in order:

            @pl.when(me != j)
            def _(j=j):
                flat_copy(group, j).start()

    def add_plane(group):
        part = part_of[group]
        others = r2.at[pl.ds(0, 31), part]
        bytes_of(others, flat_send, flat_recv.at[group]).wait_recv()
        fin[rows_of(group, c)] = jnp.sum(r2[:, part], axis=0) * (n_seq * n_grp) ** (-0.5)
        down_copy(group, 1 - c).start()
        for j in range(2, 24):
            down_copy(group, j).start()

    both(arrive_lead)
    arrive_mixed()
    send_up(0)
    arrive_one(4)
    arrive_one(5)
    send_up(1)

    for h in (lead, lead + 1, 4, 5):
        for part in range(2):
            first_copy(h, part).wait_send()
    for part in range(2):
        mixed_copy(part).wait_send()
    for h in (lack, lack + 1, 2, 3):
        for part in range(2):
            first_copy(h, part).start()
    for h in range(H):
        for part in range(2):
            second_copy(h, part).start()

    def early(i, carry):
        h = jnp.where(i < 2, lead + i, 2 + i)
        outputs(d, h)
        return carry

    lax.fori_loop(0, 4, early, 0, unroll=2)

    @pl.when(adds)
    def _():
        for group in range(2):
            add_line(group)

    for h in (lack, lack + 1, 2, 3):
        relay(h)
    for h in (lack, lack + 1):
        scores(d, h, far_row(d), 128)
    for h in (lack, lack + 1, 2, 3):
        outputs(d, h)

    def finish(i, carry):
        for h in (2 * i, 2 * i + 1):
            for part in range(2):
                relay_copy(h, part).wait_recv()
                second_copy(h, part).wait_recv()
        for h in (2 * i, 2 * i + 1):
            scores(e, h, 0, 384)
        for h in (2 * i, 2 * i + 1):
            outputs(e, h)
        return carry

    lax.fori_loop(0, H // 2, finish, 0)
    for part in range(2):
        for rest in range(2):
            chip_copy(part, rest).wait_send()
        extra_copy(part).wait_send()

    @pl.when(c == 0)
    def _():
        mask_copy(0).wait_send()

    @pl.when(c == 1)
    def _():
        mask_copy(1).wait_send()

    def drain(h, carry):
        for part in range(2):
            relay_copy(h, part).wait_send()
            second_copy(h, part).wait_send()
        return carry

    lax.fori_loop(0, H, drain, 0)
    for h in (lack, lack + 1, 2, 3):
        for part in range(2):
            first_copy(h, part).wait_send()

    @pl.when(adds)
    def _():
        for group in range(2):
            add_plane(group)
        bytes_of(r1.at[0], up_send, down_recv).wait()
        bytes_of(r2.at[pl.ds(0, 31)], flat_send, down_recv).wait_send()
        bytes_of(r1.at[pl.ds(0, 23)], down_send, down_recv).wait_send()

    @pl.when(jnp.logical_not(adds))
    def _():
        bytes_of(fin, up_send, down_recv).wait()

    for h in range(H):
        for k in range(3):
            bg_ref[h : h + 1, 128 * k : 128 * k + 128] = fin[at[h] + k]


def copy_kernel(res_ref, bg_ref, att_ref, qg_ref, kg_ref, vg_ref, bias_ref, sem):
    copies = []
    for i, (side, part, ref) in enumerate(
        ((0, 0, att_ref), (0, 1, qg_ref), (1, 1, kg_ref), (1, 0, vg_ref))
    ):
        copy = pltpu.make_async_copy(res_ref.at[side, part], ref.at[0], sem.at[i])
        copy.start()
        copies.append(copy)
    copy = pltpu.make_async_copy(bg_ref, bias_ref, sem.at[4])
    copy.start()
    copies.append(copy)
    for copy in copies:
        copy.wait()


def on_device(queries, key_rows, value_rows, out_grad, positions, user_len, position_bias):
    hbm = pl.BlockSpec(memory_space=pltpu.HBM)
    vmem = pl.BlockSpec(memory_space=pltpu.VMEM)
    dma = pltpu.SemaphoreType.DMA
    res, bg = pl.pallas_call(
        main_kernel,
        out_shape=(
            jax.ShapeDtypeStruct((2, 2, BLOCK, D), BF16),
            jax.ShapeDtypeStruct((H, 384), F32),
        ),
        in_specs=[hbm] * 7,
        out_specs=(vmem, vmem),
        scratch_shapes=[
            pltpu.VMEM((2, 2, 384, D), BF16),
            pltpu.VMEM((2, 128, D), BF16),
            pltpu.VMEM((128, 256), F32),
            pltpu.VMEM((2, 128, 256), BF16),
            pltpu.VMEM((2, 128, 256), BF16),
            pltpu.VMEM((2, H, 128, 384), F32),
            pltpu.VMEM((2, 128, 384), F32),
            pltpu.VMEM((H, 384), F32),
            pltpu.SMEM((2, 1), jnp.int32),
            pltpu.VMEM((2, H, 128, 384), BF16),
            pltpu.VMEM((2, H, 128, 384), BF16),
            pltpu.VMEM((24, 1, 128), F32),
            pltpu.VMEM((24, 12, 1, 128), F32),
            pltpu.VMEM((32, 12, 1, 128), F32),
            pltpu.VMEM((24, 1, 128), F32),
            dma((4,)),
            dma((2, 2)),
            dma((2, 2)),
            dma((2,)),
            dma((2,)),
            dma(()),
            dma(()),
            dma((2,)),
            dma((2,)),
            dma((H, 2)),
            dma((H, 2)),
            dma((H, 2)),
            dma((H, 2)),
            dma((H, 2)),
            dma((H, 2)),
            dma(()),
            dma((3,)),
            dma(()),
            dma((3,)),
            dma(()),
            dma(()),
            dma((3,)),
        ],
        compiler_params=pltpu.CompilerParams(
            collective_id=0, has_side_effects=True, vmem_limit_bytes=32 * 1024 * 1024
        ),
        name="attention",
    )(*(pltpu.with_memory_space_constraint(a, pltpu.HBM) for a in (queries, key_rows, value_rows, out_grad)), positions, user_len, pltpu.with_memory_space_constraint(position_bias, pltpu.HBM))
    whole = jax.ShapeDtypeStruct((1, BLOCK, D), BF16)
    return pl.pallas_call(
        copy_kernel,
        out_shape=(whole, whole, whole, whole, jax.ShapeDtypeStruct((H, 384), F32)),
        in_specs=[vmem, vmem],
        out_specs=(hbm,) * 5,
        scratch_shapes=[dma((5,))],
        compiler_params=pltpu.CompilerParams(vmem_limit_bytes=4 * 1024 * 1024),
        name="results",
    )(res, bg)


def solution(mesh):
    return jax.shard_map(
        on_device,
        mesh=mesh,
        in_specs=(
            P("grp", "seq", None),
            P("grp", "seq", None),
            P("grp", "seq", None),
            P("grp", "seq", None),
            P("grp", "seq"),
            P("grp", "seq"),
            P(),
        ),
        out_specs=(
            P("grp", "seq", None),
            P("grp", "seq", None),
            P("grp", "seq", None),
            P("grp", "seq", None),
            P(),
        ),
        check_vma=False,
    )
```

```python
import jax
import jax.numpy as jnp
from jax import lax
from jax.experimental import pallas as pl
from jax.experimental.pallas import tpu as pltpu
from jax.sharding import PartitionSpec as P

H = 8
BLOCK = 128
D = 1024
MESH = pl.DeviceIdType.MESH
F32 = jnp.float32
BF16 = jnp.bfloat16
SCALE = 128 ** -0.5


def own_row(side):
    return pl.multiple_of(256 * (1 - side), 128)


def far_row(side):
    return pl.multiple_of(256 * side, 128)


def head_cols(h):
    return pl.ds(pl.multiple_of(h * 128, 128), 128)


def flip(x):
    lane = lax.broadcasted_iota(jnp.int32, x.shape, 1)
    return jnp.take_along_axis(x, 127 - lane, axis=1, mode="promise_in_bounds")


def rolled(chunks, left):
    width = 128 - left
    lane = lax.broadcasted_iota(jnp.int32, (8, 128), 1)
    turned = [pltpu.roll(chunk, width, 1) for chunk in chunks]
    return [
        jnp.where(lane < width, turned[k], turned[(k + 1) % len(chunks)])
        for k in range(len(chunks))
    ]


def nt(a, b):
    return lax.dot_general(a, b, (((1,), (1,)), ((), ())), preferred_element_type=F32)


def diagonals(slopes, width, extra):
    count = width // 128
    slabs = []
    for i in range(16):
        chunks = [slopes[8 * i : 8 * i + 8, 128 * k : 128 * k + 128] for k in range(count)]
        slabs.append(rolled(chunks + [jnp.zeros((8, 128), F32)], 8 * i + extra))
    while len(slabs) > 1:
        slabs = [
            [a + b for a, b in zip(slabs[k], slabs[k + 1])] for k in range(0, len(slabs), 2)
        ]
    chunks = slabs[0]
    row = lax.broadcasted_iota(jnp.int32, (8, 128), 0)
    for bit in (1, 2, 4):
        moved = rolled(chunks, bit)
        chunks = [jnp.where((row & bit) != 0, b, a) for a, b in zip(chunks, moved)]
    return chunks


def row_sum(x):
    return jnp.sum(x, axis=0, keepdims=True)


def main_kernel(
    q_ref, k_ref, v_ref, g_ref, pos_ref, len_ref, bias_ref,
    res_ref, bg_ref,
    wide, sibling, sibling_mask, mixed_out, mixed_in, toep, mask, bias, place, wts, slp, bl, r1, r2, fin,
    load_sem, chip_send, chip_recv, extra_send, extra_recv, mask_send, mask_recv, mix_send, mix_recv, w1_send, w1_recv, rel_send, rel_recv, w2_send, w2_recv,
    up_send, up_recv, flat_send, flat_recv, down_send, down_recv, small_sem,
):
    s = lax.axis_index("seq")
    grp = lax.axis_index("grp")
    n_seq = lax.axis_size("seq")
    n_grp = lax.axis_size("grp")
    c = s % 2
    x = s // 24
    m = s % 24
    d = 1 - c
    e = c
    sib = {"seq": s + 1 - 2 * c, "grp": grp}
    ahead = {"seq": (s + 4 * c - 2 + n_seq) % n_seq, "grp": grp}
    behind = {"seq": (s + 2 - 4 * c + n_seq) % n_seq, "grp": grp}

    barrier = pltpu.get_barrier_semaphore()

    def greet(device):
        pl.semaphore_signal(barrier, inc=1, device_id=device, device_id_type=MESH)

    def line_peer(j):
        return {"seq": s - m + j, "grp": grp}

    def plane_peer(j):
        t = (x * n_grp + grp + j) % 32
        return {"seq": (t // n_grp) * 24 + m, "grp": t % n_grp}

    adds = m == 1
    greet(ahead)
    greet(behind)
    greet(sib)

    loads = []
    for i, (ref, side, part) in enumerate(
        ((q_ref, 1, 0), (g_ref, 1, 1), (k_ref, 0, 0), (v_ref, 0, 1))
    ):
        row = 256 * (1 - side)
        copy = pltpu.make_async_copy(
            ref.at[0], wide.at[side, part, pl.ds(row, 128)], load_sem.at[i]
        )
        copy.start()
        loads.append(copy)

    smalls = []
    for i, (src, dst) in enumerate(
        ((bias_ref, bias), (pos_ref, place.at[pl.ds(0, 1)]), (len_ref, place.at[pl.ds(1, 1)]))
    ):
        copy = pltpu.make_async_copy(src, dst, small_sem.at[i])
        copy.start()
        smalls.append(copy)
    @pl.when(adds)
    def _():
        for j in range(1, 32):
            greet(plane_peer(j))
        for j in range(2, 24):
            greet(line_peer(j))

    for copy in loads:
        copy.wait()

    @pl.when(adds)
    def _():
        pl.semaphore_wait(barrier, 3 + 31)

    @pl.when(m == 0)
    def _():
        pl.semaphore_wait(barrier, 3)

    @pl.when(m > 1)
    def _():
        pl.semaphore_wait(barrier, 3 + 1)

    def piece(side, part, rows, h):
        return wide.at[side, part, pl.ds(rows, 128), head_cols(h)]

    def first_copy(h, part):
        return pltpu.make_async_remote_copy(
            src_ref=piece(d, part, own_row(d), h), dst_ref=piece(d, part, far_row(d), h),
            send_sem=w1_send.at[h, part], recv_sem=w1_recv.at[h, part],
            device_id=ahead, device_id_type=MESH,
        )

    def pair_copy(h, part):
        cols = pl.ds(pl.multiple_of(h * 128, 128), 256)
        return pltpu.make_async_remote_copy(
            src_ref=wide.at[d, part, pl.ds(own_row(d), 128), cols],
            dst_ref=wide.at[d, part, pl.ds(far_row(d), 128), cols],
            send_sem=w1_send.at[h, part], recv_sem=w1_recv.at[h, part],
            device_id=ahead, device_id_type=MESH,
        )

    def second_copy(i, part):
        cols = pl.ds(512 * i, 512)
        return pltpu.make_async_remote_copy(
            src_ref=wide.at[e, part, pl.ds(own_row(e), 128), cols],
            dst_ref=wide.at[e, part, pl.ds(far_row(e), 128), cols],
            send_sem=w2_send.at[i, part], recv_sem=w2_recv.at[i, part],
            device_id=behind, device_id_type=MESH,
        )

    def relay_copy(h, part):
        return pltpu.make_async_remote_copy(
            src_ref=piece(d, part, far_row(d), h), dst_ref=piece(d, part, 128, h),
            send_sem=rel_send.at[h, part], recv_sem=rel_recv.at[h, part],
            device_id=sib, device_id_type=MESH,
        )

    def chip_copy(part, rest):
        cols = pl.ds(pl.multiple_of(256 * (1 - c), 128), 768) if rest else pl.ds(pl.multiple_of(768 * c, 128), 256)
        return pltpu.make_async_remote_copy(
            src_ref=wide.at[e, part, pl.ds(own_row(e), 128), cols],
            dst_ref=wide.at[e, part, pl.ds(128, 128), cols],
            send_sem=chip_send.at[part, rest], recv_sem=chip_recv.at[part, rest],
            device_id=sib, device_id_type=MESH,
        )

    def extra_copy(part):
        return pltpu.make_async_remote_copy(
            src_ref=wide.at[d, part, pl.ds(own_row(d), 128)], dst_ref=sibling.at[part],
            send_sem=extra_send.at[part], recv_sem=extra_recv.at[part],
            device_id=sib, device_id_type=MESH,
        )

    def mixed_copy(part):
        return pltpu.make_async_remote_copy(
            src_ref=mixed_out.at[part], dst_ref=mixed_in.at[part],
            send_sem=mix_send.at[part], recv_sem=mix_recv.at[part],
            device_id=ahead, device_id_type=MESH,
        )

    def mask_copy(core):
        if core == 0:
            src, dst = mask.at[0, :, pl.ds(0, 256)], sibling_mask
        else:
            src, dst = mask.at[1, pl.ds(0, 8), pl.ds(128, 256)], sibling_mask.at[pl.ds(0, 8)]
        return pltpu.make_async_remote_copy(
            src_ref=src, dst_ref=dst, send_sem=mask_send, recv_sem=mask_recv,
            device_id=sib, device_id_type=MESH,
        )

    lead = 6 - 6 * c
    lack = 6 * c
    for part in range(2):
        chip_copy(part, 0).start()
    for h in (lead, lead + 1):
        first_copy(h, 0).start()
        first_copy(h, 1).start()
    for part in range(2):
        chip_copy(part, 1).start()
    for part in range(2):
        extra_copy(part).start()

    for copy in smalls:
        copy.wait()
    p = place[0, 0]
    n = place[1, 0]
    row = lax.broadcasted_iota(jnp.int32, (128, 384), 0)
    lane = lax.broadcasted_iota(jnp.int32, (128, 384), 1)
    inverse = 1.0 / jnp.full((128, 384), n, jnp.int32).astype(F32)
    used = (row < n - p * 128) & (lane >= 256 - 128 * p) & (lane <= 256 + row)
    mask[0] = jnp.where(used, inverse, 0.0)
    used = (lane < n - p * 128) & (lane >= row)
    mask[1] = jnp.where(used, inverse, 0.0)

    for part in range(2):
        chip_copy(part, 0).wait_recv()
    use_sibling = jnp.where(p == 1, 1, 0) * jnp.where(n > 256, 1, 0)
    for part in range(2):
        theirs = wide[d, part, pl.ds(128, 128), pl.ds(pl.multiple_of(128 * lead, 128), 256)]
        mine = wide[d, part, pl.ds(own_row(d), 128), pl.ds(256, 256)]
        mixed_out[part] = jnp.where(use_sibling == 1, theirs, mine)
        mixed_copy(part).start()
    for h in (4, 5):
        first_copy(h, 0).start()
        first_copy(h, 1).start()

    @pl.when(c == 0)
    def _():
        mask_copy(0).start()

    @pl.when(c == 1)
    def _():
        mask_copy(1).start()

    def make_toep(side):
        def body(h, carry):
            b = jnp.broadcast_to(bias[pl.ds(h, 1), :] * 0.5, (8, 384))
            b0, b1, b2 = b[:, :128], b[:, 128:256], b[:, 256:]
            zero = jnp.zeros_like(b0)
            keyed = jnp.concatenate([b0, b1, b2, zero], axis=1)
            back = jnp.concatenate([flip(b1), flip(b0), zero, flip(b2)], axis=1)
            base = jnp.where(side == 1, keyed, pltpu.roll(back, 1, 1))
            base = jnp.broadcast_to(base[0:1], (128, 512))
            toep[side, h] = pltpu.roll(base, 0, 1, stride=1, stride_axis=0)[:, :384]
            return carry

        lax.fori_loop(0, H, body, 0, unroll=2)


    make_toep(d)

    def entries(x, y, x3, y3, near, mk):
        z = nt(x, x3) * (0.5 * SCALE) + near
        pulled = nt(y, y3)
        t = jnp.tanh(z)
        w0 = z * t + z
        sg = 0.5 * t + 0.5
        return w0 * mk, pulled * (sg + w0 * (1.0 - sg)) * mk

    def scores(side, h, lo, width, moved=None):
        cols = head_cols(h)
        rows = pl.ds(lo, width)
        other = 1 - side
        own = pl.ds(own_row(other), 128)
        x3, y3 = (wide[side, 0, rows, cols], wide[side, 1, rows, cols]) if moved is None else moved
        weights, slopes = entries(
            wide[other, 0, own, cols], wide[other, 1, own, cols], x3, y3,
            toep[side, h, :, rows], mask[side, :, rows],
        )
        wts[side, h, :, rows] = weights.astype(BF16)
        slp[side, h, :, rows] = slopes.astype(BF16)
        return slopes

    def sibling_scores(side, h, lo, x3, y3, mk):
        cols = head_cols(h)
        return entries(sibling[0, :, cols], sibling[1, :, cols], x3, y3, toep[side, h, :, lo : lo + 128], mk)[1]

    def outputs(side, h):
        cols = head_cols(h)
        o1 = jnp.dot(wts[side, h], wide[side, 1, :, cols], preferred_element_type=F32)
        o2 = jnp.dot(slp[side, h], wide[side, 0, :, cols], preferred_element_type=F32)
        res_ref[side, 0, :, cols] = o1.astype(BF16)
        res_ref[side, 1, :, cols] = (o2 * SCALE).astype(BF16)

    first_core = c == 0
    at = (0, 3, 6, 9, 18, 21, 12, 15)

    def count(h, offset, slopes, turned):
        f0, f1 = diagonals(slopes, 128, 1 if turned else 0)
        low, high = (flip(f0), flip(f1)) if turned else (f1, f0)
        k = at[h] + offset - 1
        bl[k] = bl[k] + row_sum(low)
        bl[k + 1] = bl[k + 1] + row_sum(high)

    for part in range(2):
        chip_copy(part, 1).wait_recv()

    def direct_near(h):
        slopes = scores(d, h, pl.multiple_of(128 * (1 - d), 128), 256)
        lanes = lax.broadcasted_iota(jnp.int32, (128, 256), 1)
        slopes = jnp.where(first_core | (lanes >= 128), slopes, 0.0)
        n0, n1, _ = diagonals(slopes, 256, c)
        bl[at[h]] = row_sum(jnp.where(first_core, n0, flip(n0)))
        bl[at[h] + 1] = row_sum(jnp.where(first_core, n1, 0.0))
        bl[at[h] + 2] = jnp.zeros((1, 128), F32)

    for h in range(H):
        direct_near(h)

    for part in range(2):
        extra_copy(part).wait_recv()

    @pl.when(c == 0)
    def _():
        mask_copy(1).wait_recv()

    @pl.when(c == 1)
    def _():
        mask_copy(0).wait_recv()

    def relay(h):
        for part in range(2):
            first_copy(h, part).wait_recv()
            relay_copy(h, part).start()

    def far_pairs(h, turned, siblings):
        cols = head_cols(h)
        if turned:
            count(h, 2, scores(0, h, 0, 128), True)
            if siblings:
                mk = sibling_mask[:, 128:]
                count(h, 1, sibling_scores(0, h, 128, wide[0, 0, :128, cols], wide[0, 1, :128, cols], mk), True)
        else:
            count(h, 2, scores(1, h, 256, 128), False)
            mk = sibling_mask[0:1, :128]
            count(h, 1, sibling_scores(1, h, 128, wide[1, 0, 256:, cols], wide[1, 1, 256:, cols], mk), False)

    def mixed_pairs(turned):
        for i in range(2):
            moved = tuple(mixed_in[part, :, 128 * i : 128 * i + 128] for part in range(2))
            if turned:
                count(2 + i, 2, scores(0, 2 + i, 0, 128, moved), True)
                third = sibling_mask[:, :128]
                count(i, 2, sibling_scores(0, i, 0, *moved, third), True)
                second = jnp.where(third > 0.0, 0.0, sibling_mask[:, 128:])
                count(2 + i, 1, sibling_scores(0, 2 + i, 128, *moved, second), True)
            else:
                count(2 + i, 2, scores(1, 2 + i, 256, 128, moved), False)
                second = jnp.where(mask[1, 0:1, 256:] > 0.0, sibling_mask[0:1, :128], 0.0)
                count(2 + i, 1, sibling_scores(1, 2 + i, 128, *moved, second), False)
                third = sibling_mask[0:1, 128:]
                count(6 + i, 2, sibling_scores(1, 6 + i, 256, *moved, third), False)

    def both(todo):
        @pl.when(c == 0)
        def _():
            todo(False)

        @pl.when(c == 1)
        def _():
            todo(True)

    def arrive_lead(turned):
        for h in (0, 1) if turned else (6, 7):
            relay(h)
        for h in (0, 1) if turned else (6, 7):
            far_pairs(h, turned, True)

    def arrive_one(h):
        relay(h)
        both(lambda turned: far_pairs(h, turned, False))

    def arrive_mixed():
        for part in range(2):
            mixed_copy(part).wait_recv()
        both(mixed_pairs)

    me = x * n_grp + grp
    order = [8 * i + j for j in (0, 1, 2, 3, 7, 6, 4, 5) for i in (0, 2, 3, 1)]
    part_of = (pl.ds(0, 18), pl.ds(18, 6))

    def up_copy(group):
        part = part_of[group]
        return pltpu.make_async_remote_copy(
            src_ref=bl.at[part], dst_ref=r1.at[m, part],
            send_sem=up_send, recv_sem=up_recv.at[group],
            device_id=line_peer(1), device_id_type=MESH,
        )

    def flat_copy(group, j):
        part = part_of[group]
        return pltpu.make_async_remote_copy(
            src_ref=r2.at[me, part], dst_ref=r2.at[me, part],
            send_sem=flat_send, recv_sem=flat_recv.at[group],
            device_id={"seq": (j // 8) * 24 + m, "grp": j % 8}, device_id_type=MESH,
        )

    def down_copy(group, j):
        part = part_of[group]
        return pltpu.make_async_remote_copy(
            src_ref=fin.at[part], dst_ref=fin.at[part],
            send_sem=down_send, recv_sem=down_recv,
            device_id=line_peer(j), device_id_type=MESH,
        )

    def bytes_of(ref, send_sem, recv_sem):
        return pltpu.make_async_remote_copy(
            src_ref=ref, dst_ref=ref, send_sem=send_sem, recv_sem=recv_sem,
            device_id=sib, device_id_type=MESH,
        )

    def send_up(group):
        @pl.when(adds)
        def _():
            r1[m, part_of[group]] = bl[part_of[group]]

        @pl.when(jnp.logical_not(adds))
        def _():
            up_copy(group).start()

    def add_line(group):
        part = part_of[group]
        bytes_of(r1.at[pl.ds(0, 23), part], up_send, up_recv.at[group]).wait_recv()
        r2[me, part] = jnp.sum(r1[:, part], axis=0)
        for j in order:

            @pl.when(me != j)
            def _(j=j):
                flat_copy(group, j).start()

    def add_plane(group):
        part = part_of[group]
        bytes_of(r2.at[pl.ds(0, 31), part], flat_send, flat_recv.at[group]).wait_recv()
        fin[part] = jnp.sum(r2[:, part], axis=0) * (n_seq * n_grp) ** (-0.5)
        for j in (0, *range(2, 6)):
            down_copy(group, j).start()

        @pl.when((me > 0) | (group == 0))
        def _():
            for j in range(6, 24):
                down_copy(group, j).start()

    both(arrive_lead)
    arrive_mixed()
    send_up(0)
    arrive_one(4)

    arrive_one(5)
    send_up(1)

    for h in (lack, 2):
        for part in range(2):
            pair_copy(h, part).start()
    for i in range(2):
        for part in range(2):
            second_copy(i, part).start()

    make_toep(e)

    def early(i, carry):
        h = jnp.where(i < 2, lead + i, 2 + i)
        outputs(d, h)
        return carry

    lax.fori_loop(0, 4, early, 0, unroll=2)

    @pl.when(adds)
    def _():
        for group in range(2):
            add_line(group)

    for h in (lack, 2):
        for part in range(2):
            pair_copy(h, part).wait_recv()
            relay_copy(h, part).start()
            relay_copy(h + 1, part).start()
    for h in (lack, lack + 1):
        scores(d, h, far_row(d), 128)
    for h in (lack, lack + 1, 2, 3):
        outputs(d, h)

    for i in range(2):
        heads = range(4 * i, 4 * i + 4)
        for part in range(2):
            for h in heads:
                relay_copy(h, part).wait_recv()
            second_copy(i, part).wait_recv()
        for h in heads:
            scores(e, h, 0, 384)
        for h in heads:
            outputs(e, h)
    for part in range(2):
        for rest in range(2):
            chip_copy(part, rest).wait_send()
        extra_copy(part).wait_send()

    @pl.when(c == 0)
    def _():
        mask_copy(0).wait_send()

    @pl.when(c == 1)
    def _():
        mask_copy(1).wait_send()

    def drain(h, carry):
        for part in range(2):
            relay_copy(h, part).wait_send()
        return carry

    lax.fori_loop(0, H, drain, 0)
    for part in range(2):
        for h in (lead, lead + 1, 4, 5):
            first_copy(h, part).wait_send()
        mixed_copy(part).wait_send()
        for h in (lack, 2):
            pair_copy(h, part).wait_send()
        for i in range(2):
            second_copy(i, part).wait_send()

    @pl.when(adds)
    def _():
        for group in range(2):
            add_plane(group)
        bytes_of(r2.at[pl.ds(0, 31)], flat_send, down_recv).wait_send()
        bytes_of(r1.at[pl.ds(0, 23), part_of[0]], down_send, down_recv).wait_send()
        bytes_of(r1.at[pl.ds(0, 5), part_of[1]], down_send, down_recv).wait_send()

        @pl.when(me > 0)
        def _():
            bytes_of(r1.at[pl.ds(0, 18), part_of[1]], down_send, down_recv).wait_send()

    @pl.when(jnp.logical_not(adds))
    def _():
        bytes_of(fin, up_send, down_recv).wait()

    @pl.when((m == 0) & (me == 0))
    def _():
        for j in range(6, 24):
            down_copy(1, j).start()
        bytes_of(r1.at[pl.ds(0, 18), part_of[1]], down_send, down_recv).wait_send()

    for h in range(H):
        for k in range(3):
            bg_ref[h : h + 1, 128 * k : 128 * k + 128] = fin[at[h] + k]


def copy_kernel(res_ref, bg_ref, att_ref, qg_ref, kg_ref, vg_ref, bias_ref, sem):
    copies = []
    for i, (side, part, ref) in enumerate(
        ((0, 0, att_ref), (0, 1, qg_ref), (1, 1, kg_ref), (1, 0, vg_ref))
    ):
        copy = pltpu.make_async_copy(res_ref.at[side, part], ref.at[0], sem.at[i])
        copy.start()
        copies.append(copy)
    copy = pltpu.make_async_copy(bg_ref, bias_ref, sem.at[4])
    copy.start()
    copies.append(copy)
    for copy in copies:
        copy.wait()


def on_device(queries, key_rows, value_rows, out_grad, positions, user_len, position_bias):
    hbm = pl.BlockSpec(memory_space=pltpu.HBM)
    vmem = pl.BlockSpec(memory_space=pltpu.VMEM)
    dma = pltpu.SemaphoreType.DMA
    res, bg = pl.pallas_call(
        main_kernel,
        out_shape=(
            jax.ShapeDtypeStruct((2, 2, BLOCK, D), BF16),
            jax.ShapeDtypeStruct((H, 384), F32),
        ),
        in_specs=[hbm] * 7,
        out_specs=(vmem, vmem),
        scratch_shapes=[
            pltpu.VMEM((2, 2, 384, D), BF16),
            pltpu.VMEM((2, 128, D), BF16),
            pltpu.VMEM((128, 256), F32),
            pltpu.VMEM((2, 128, 256), BF16),
            pltpu.VMEM((2, 128, 256), BF16),
            pltpu.VMEM((2, H, 128, 384), F32),
            pltpu.VMEM((2, 128, 384), F32),
            pltpu.VMEM((H, 384), F32),
            pltpu.SMEM((2, 1), jnp.int32),
            pltpu.VMEM((2, H, 128, 384), BF16),
            pltpu.VMEM((2, H, 128, 384), BF16),
            pltpu.VMEM((24, 1, 128), F32),
            pltpu.VMEM((24, 24, 1, 128), F32),
            pltpu.VMEM((32, 24, 1, 128), F32),
            pltpu.VMEM((24, 1, 128), F32),
            dma((4,)),
            dma((2, 2)),
            dma((2, 2)),
            dma((2,)),
            dma((2,)),
            dma(()),
            dma(()),
            dma((2,)),
            dma((2,)),
            dma((H, 2)),
            dma((H, 2)),
            dma((H, 2)),
            dma((H, 2)),
            dma((H, 2)),
            dma((H, 2)),
            dma(()),
            dma((3,)),
            dma(()),
            dma((3,)),
            dma(()),
            dma(()),
            dma((3,)),
        ],
        compiler_params=pltpu.CompilerParams(
            collective_id=0, has_side_effects=True, vmem_limit_bytes=32 * 1024 * 1024
        ),
        name="attention",
    )(*(pltpu.with_memory_space_constraint(a, pltpu.HBM) for a in (queries, key_rows, value_rows, out_grad)), positions, user_len, pltpu.with_memory_space_constraint(position_bias, pltpu.HBM))
    whole = jax.ShapeDtypeStruct((1, BLOCK, D), BF16)
    return pl.pallas_call(
        copy_kernel,
        out_shape=(whole, whole, whole, whole, jax.ShapeDtypeStruct((H, 384), F32)),
        in_specs=[vmem, vmem],
        out_specs=(hbm,) * 5,
        scratch_shapes=[dma((5,))],
        compiler_params=pltpu.CompilerParams(vmem_limit_bytes=4 * 1024 * 1024),
        name="results",
    )(res, bg)


def solution(mesh):
    return jax.shard_map(
        on_device,
        mesh=mesh,
        in_specs=(
            P("grp", "seq", None),
            P("grp", "seq", None),
            P("grp", "seq", None),
            P("grp", "seq", None),
            P("grp", "seq"),
            P("grp", "seq"),
            P(),
        ),
        out_specs=(
            P("grp", "seq", None),
            P("grp", "seq", None),
            P("grp", "seq", None),
            P("grp", "seq", None),
            P(),
        ),
        check_vma=False,
    )
```

```python
import jax
import jax.numpy as jnp
from jax import lax
from jax.experimental import pallas as pl
from jax.experimental.pallas import tpu as pltpu
from jax.sharding import PartitionSpec as P

H = 8
BLOCK = 128
D = 1024
MESH = pl.DeviceIdType.MESH
F32 = jnp.float32
BF16 = jnp.bfloat16
SCALE = 128 ** -0.5


def own_row(side):
    return pl.multiple_of(256 * (1 - side), 128)


def far_row(side):
    return pl.multiple_of(256 * side, 128)


def head_cols(h):
    return pl.ds(pl.multiple_of(h * 128, 128), 128)


def flip(x):
    lane = lax.broadcasted_iota(jnp.int32, x.shape, 1)
    return jnp.take_along_axis(x, 127 - lane, axis=1, mode="promise_in_bounds")


def rolled(chunks, left):
    width = 128 - left
    lane = lax.broadcasted_iota(jnp.int32, (8, 128), 1)
    turned = [pltpu.roll(chunk, width, 1) for chunk in chunks]
    return [
        jnp.where(lane < width, turned[k], turned[(k + 1) % len(chunks)])
        for k in range(len(chunks))
    ]


def nt(a, b):
    return lax.dot_general(a, b, (((1,), (1,)), ((), ())), preferred_element_type=F32)


def diagonals(slopes, width, extra):
    count = width // 128
    slabs = []
    for i in range(16):
        chunks = [slopes[8 * i : 8 * i + 8, 128 * k : 128 * k + 128] for k in range(count)]
        slabs.append(rolled(chunks + [jnp.zeros((8, 128), F32)], 8 * i + extra))
    while len(slabs) > 1:
        slabs = [
            [a + b for a, b in zip(slabs[k], slabs[k + 1])] for k in range(0, len(slabs), 2)
        ]
    chunks = slabs[0]
    row = lax.broadcasted_iota(jnp.int32, (8, 128), 0)
    for bit in (1, 2, 4):
        moved = rolled(chunks, bit)
        chunks = [jnp.where((row & bit) != 0, b, a) for a, b in zip(chunks, moved)]
    return chunks


def row_sum(x):
    return jnp.sum(x, axis=0, keepdims=True)


def main_kernel(
    q_ref, k_ref, v_ref, g_ref, pos_ref, len_ref, bias_ref,
    res_ref, bg_ref,
    wide, sibling, sibling_mask, mixed_out, mixed_in, toep, mask, bias, place, wts, slp, bl, r1, r2, fin,
    load_sem, chip_send, chip_recv, extra_send, extra_recv, mask_send, mask_recv, mix_send, mix_recv, w1_send, w1_recv, rel_send, rel_recv, w2_send, w2_recv,
    up_send, up_recv, flat_send, flat_recv, down_send, down_recv, small_sem,
):
    s = lax.axis_index("seq")
    grp = lax.axis_index("grp")
    n_seq = lax.axis_size("seq")
    n_grp = lax.axis_size("grp")
    c = s % 2
    x = s // 24
    m = s % 24
    d = 1 - c
    e = c
    sib = {"seq": s + 1 - 2 * c, "grp": grp}
    ahead = {"seq": (s + 4 * c - 2 + n_seq) % n_seq, "grp": grp}
    behind = {"seq": (s + 2 - 4 * c + n_seq) % n_seq, "grp": grp}

    barrier = pltpu.get_barrier_semaphore()

    def greet(device):
        pl.semaphore_signal(barrier, inc=1, device_id=device, device_id_type=MESH)

    def line_peer(j):
        return {"seq": s - m + j, "grp": grp}

    def plane_peer(j):
        t = (x * n_grp + grp + j) % 32
        return {"seq": (t // n_grp) * 24 + m, "grp": t % n_grp}

    adds = m == 1
    greet(ahead)
    greet(behind)
    greet(sib)

    loads = []
    for i, (ref, side, part) in enumerate(
        ((q_ref, 1, 0), (g_ref, 1, 1), (k_ref, 0, 0), (v_ref, 0, 1))
    ):
        row = 256 * (1 - side)
        copy = pltpu.make_async_copy(
            ref.at[0], wide.at[side, part, pl.ds(row, 128)], load_sem.at[i]
        )
        copy.start()
        loads.append(copy)

    smalls = []
    for i, (src, dst) in enumerate(
        ((bias_ref, bias), (pos_ref, place.at[pl.ds(0, 1)]), (len_ref, place.at[pl.ds(1, 1)]))
    ):
        copy = pltpu.make_async_copy(src, dst, small_sem.at[i])
        copy.start()
        smalls.append(copy)
    @pl.when(adds)
    def _():
        for j in range(1, 32):
            greet(plane_peer(j))
        for j in range(2, 24):
            greet(line_peer(j))

    for copy in loads:
        copy.wait()

    @pl.when(adds)
    def _():
        pl.semaphore_wait(barrier, 3 + 31)

    @pl.when(m == 0)
    def _():
        pl.semaphore_wait(barrier, 3)

    @pl.when(m > 1)
    def _():
        pl.semaphore_wait(barrier, 3 + 1)

    def piece(side, part, rows, h):
        return wide.at[side, part, pl.ds(rows, 128), head_cols(h)]

    def first_copy(h, part):
        return pltpu.make_async_remote_copy(
            src_ref=piece(d, part, own_row(d), h), dst_ref=piece(d, part, far_row(d), h),
            send_sem=w1_send.at[h, part], recv_sem=w1_recv.at[h, part],
            device_id=ahead, device_id_type=MESH,
        )

    def pair_copy(h, part):
        cols = pl.ds(pl.multiple_of(h * 128, 128), 256)
        return pltpu.make_async_remote_copy(
            src_ref=wide.at[d, part, pl.ds(own_row(d), 128), cols],
            dst_ref=wide.at[d, part, pl.ds(far_row(d), 128), cols],
            send_sem=w1_send.at[h, part], recv_sem=w1_recv.at[h, part],
            device_id=ahead, device_id_type=MESH,
        )

    def second_copy(i, part):
        cols = pl.ds(512 * i, 512)
        return pltpu.make_async_remote_copy(
            src_ref=wide.at[e, part, pl.ds(own_row(e), 128), cols],
            dst_ref=wide.at[e, part, pl.ds(far_row(e), 128), cols],
            send_sem=w2_send.at[i, part], recv_sem=w2_recv.at[i, part],
            device_id=behind, device_id_type=MESH,
        )

    def relay_copy(h, part):
        return pltpu.make_async_remote_copy(
            src_ref=piece(d, part, far_row(d), h), dst_ref=piece(d, part, 128, h),
            send_sem=rel_send.at[h, part], recv_sem=rel_recv.at[h, part],
            device_id=sib, device_id_type=MESH,
        )

    def chip_copy(part, rest):
        cols = pl.ds(pl.multiple_of(256 * (1 - c), 128), 768) if rest else pl.ds(pl.multiple_of(768 * c, 128), 256)
        return pltpu.make_async_remote_copy(
            src_ref=wide.at[e, part, pl.ds(own_row(e), 128), cols],
            dst_ref=wide.at[e, part, pl.ds(128, 128), cols],
            send_sem=chip_send.at[part, rest], recv_sem=chip_recv.at[part, rest],
            device_id=sib, device_id_type=MESH,
        )

    def extra_copy(part):
        return pltpu.make_async_remote_copy(
            src_ref=wide.at[d, part, pl.ds(own_row(d), 128)], dst_ref=sibling.at[part],
            send_sem=extra_send.at[part], recv_sem=extra_recv.at[part],
            device_id=sib, device_id_type=MESH,
        )

    def mixed_copy(part):
        return pltpu.make_async_remote_copy(
            src_ref=mixed_out.at[part], dst_ref=mixed_in.at[part],
            send_sem=mix_send.at[part], recv_sem=mix_recv.at[part],
            device_id=ahead, device_id_type=MESH,
        )

    def mask_copy(core):
        if core == 0:
            src, dst = mask.at[0, :, pl.ds(0, 256)], sibling_mask
        else:
            src, dst = mask.at[1, pl.ds(0, 8), pl.ds(128, 256)], sibling_mask.at[pl.ds(0, 8)]
        return pltpu.make_async_remote_copy(
            src_ref=src, dst_ref=dst, send_sem=mask_send, recv_sem=mask_recv,
            device_id=sib, device_id_type=MESH,
        )

    lead = 6 - 6 * c
    lack = 6 * c
    for part in range(2):
        chip_copy(part, 0).start()
    for h in (lead, lead + 1):
        first_copy(h, 0).start()
        first_copy(h, 1).start()
    for part in range(2):
        chip_copy(part, 1).start()
    for part in range(2):
        extra_copy(part).start()

    for copy in smalls:
        copy.wait()
    p = place[0, 0]
    n = place[1, 0]
    row = lax.broadcasted_iota(jnp.int32, (128, 384), 0)
    lane = lax.broadcasted_iota(jnp.int32, (128, 384), 1)
    inverse = 1.0 / jnp.full((128, 384), n, jnp.int32).astype(F32)
    used = (row < n - p * 128) & (lane >= 256 - 128 * p) & (lane <= 256 + row)
    mask[0] = jnp.where(used, inverse, 0.0)
    used = (lane < n - p * 128) & (lane >= row)
    mask[1] = jnp.where(used, inverse, 0.0)

    for part in range(2):
        chip_copy(part, 0).wait_recv()
    use_sibling = jnp.where(p == 1, 1, 0) * jnp.where(n > 256, 1, 0)
    for part in range(2):
        theirs = wide[d, part, pl.ds(128, 128), pl.ds(pl.multiple_of(128 * lead, 128), 256)]
        mine = wide[d, part, pl.ds(own_row(d), 128), pl.ds(256, 256)]
        mixed_out[part] = jnp.where(use_sibling == 1, theirs, mine)
        mixed_copy(part).start()
    for h in (4, 5):
        first_copy(h, 0).start()
        first_copy(h, 1).start()

    @pl.when(c == 0)
    def _():
        mask_copy(0).start()

    @pl.when(c == 1)
    def _():
        mask_copy(1).start()

    def make_toep(side):
        def body(h, carry):
            b = jnp.broadcast_to(bias[pl.ds(h, 1), :] * 0.5, (8, 384))
            b0, b1, b2 = b[:, :128], b[:, 128:256], b[:, 256:]
            zero = jnp.zeros_like(b0)
            keyed = jnp.concatenate([b0, b1, b2, zero], axis=1)
            back = jnp.concatenate([flip(b1), flip(b0), zero, flip(b2)], axis=1)
            base = jnp.where(side == 1, keyed, pltpu.roll(back, 1, 1))
            base = jnp.broadcast_to(base[0:1], (128, 512))
            toep[side, h] = pltpu.roll(base, 0, 1, stride=1, stride_axis=0)[:, :384]
            return carry

        lax.fori_loop(0, H, body, 0, unroll=2)


    make_toep(d)

    def entries(x, y, x3, y3, near, mk):
        z = nt(x, x3) * (0.5 * SCALE) + near
        pulled = nt(y, y3)
        t = jnp.tanh(z)
        w0 = z * t + z
        sg = 0.5 * t + 0.5
        return w0 * mk, pulled * (sg + w0 * (1.0 - sg)) * mk

    def scores(side, h, lo, width, moved=None):
        cols = head_cols(h)
        rows = pl.ds(lo, width)
        other = 1 - side
        own = pl.ds(own_row(other), 128)
        x3, y3 = (wide[side, 0, rows, cols], wide[side, 1, rows, cols]) if moved is None else moved
        weights, slopes = entries(
            wide[other, 0, own, cols], wide[other, 1, own, cols], x3, y3,
            toep[side, h, :, rows], mask[side, :, rows],
        )
        wts[side, h, :, rows] = weights.astype(BF16)
        slp[side, h, :, rows] = slopes.astype(BF16)
        return slopes

    def sibling_scores(side, h, lo, x3, y3, mk):
        cols = head_cols(h)
        return entries(sibling[0, :, cols], sibling[1, :, cols], x3, y3, toep[side, h, :, lo : lo + 128], mk)[1]

    def outputs(side, h):
        cols = head_cols(h)
        o1 = jnp.dot(wts[side, h], wide[side, 1, :, cols], preferred_element_type=F32)
        o2 = jnp.dot(slp[side, h], wide[side, 0, :, cols], preferred_element_type=F32)
        res_ref[side, 0, :, cols] = o1.astype(BF16)
        res_ref[side, 1, :, cols] = (o2 * SCALE).astype(BF16)

    first_core = c == 0
    at = (0, 3, 6, 9, 18, 21, 12, 15)

    def count(h, offset, slopes, turned):
        f0, f1 = diagonals(slopes, 128, 1 if turned else 0)
        low, high = (flip(f0), flip(f1)) if turned else (f1, f0)
        k = at[h] + offset - 1
        bl[k] = bl[k] + row_sum(low)
        bl[k + 1] = bl[k + 1] + row_sum(high)

    for part in range(2):
        chip_copy(part, 1).wait_recv()

    def direct_near(h):
        slopes = scores(d, h, pl.multiple_of(128 * (1 - d), 128), 256)
        lanes = lax.broadcasted_iota(jnp.int32, (128, 256), 1)
        slopes = jnp.where(first_core | (lanes >= 128), slopes, 0.0)
        n0, n1, _ = diagonals(slopes, 256, c)
        bl[at[h]] = row_sum(jnp.where(first_core, n0, flip(n0)))
        bl[at[h] + 1] = row_sum(jnp.where(first_core, n1, 0.0))
        bl[at[h] + 2] = jnp.zeros((1, 128), F32)

    for h in range(H):
        direct_near(h)

    for part in range(2):
        extra_copy(part).wait_recv()

    @pl.when(c == 0)
    def _():
        mask_copy(1).wait_recv()

    @pl.when(c == 1)
    def _():
        mask_copy(0).wait_recv()

    def relay(h):
        for part in range(2):
            first_copy(h, part).wait_recv()
            relay_copy(h, part).start()

    def far_pairs(h, turned, siblings):
        cols = head_cols(h)
        if turned:
            count(h, 2, scores(0, h, 0, 128), True)
            if siblings:
                mk = sibling_mask[:, 128:]
                count(h, 1, sibling_scores(0, h, 128, wide[0, 0, :128, cols], wide[0, 1, :128, cols], mk), True)
        else:
            count(h, 2, scores(1, h, 256, 128), False)
            mk = sibling_mask[0:1, :128]
            count(h, 1, sibling_scores(1, h, 128, wide[1, 0, 256:, cols], wide[1, 1, 256:, cols], mk), False)

    def mixed_pairs(turned):
        for i in range(2):
            moved = tuple(mixed_in[part, :, 128 * i : 128 * i + 128] for part in range(2))
            if turned:
                count(2 + i, 2, scores(0, 2 + i, 0, 128, moved), True)
                third = sibling_mask[:, :128]
                count(i, 2, sibling_scores(0, i, 0, *moved, third), True)
                second = jnp.where(third > 0.0, 0.0, sibling_mask[:, 128:])
                count(2 + i, 1, sibling_scores(0, 2 + i, 128, *moved, second), True)
            else:
                count(2 + i, 2, scores(1, 2 + i, 256, 128, moved), False)
                second = jnp.where(mask[1, 0:1, 256:] > 0.0, sibling_mask[0:1, :128], 0.0)
                count(2 + i, 1, sibling_scores(1, 2 + i, 128, *moved, second), False)
                third = sibling_mask[0:1, 128:]
                count(6 + i, 2, sibling_scores(1, 6 + i, 256, *moved, third), False)

    def both(todo):
        @pl.when(c == 0)
        def _():
            todo(False)

        @pl.when(c == 1)
        def _():
            todo(True)

    def arrive_lead(turned):
        for h in (0, 1) if turned else (6, 7):
            relay(h)
        for h in (0, 1) if turned else (6, 7):
            far_pairs(h, turned, True)

    def arrive_one(h):
        relay(h)
        both(lambda turned: far_pairs(h, turned, False))

    def arrive_mixed():
        for part in range(2):
            mixed_copy(part).wait_recv()
        both(mixed_pairs)

    me = x * n_grp + grp
    order = [8 * i + j for j in (0, 1, 2, 3, 7, 6, 4, 5) for i in (0, 2, 3, 1)]
    part_of = (pl.ds(0, 18), pl.ds(18, 6))

    def up_copy(group):
        part = part_of[group]
        return pltpu.make_async_remote_copy(
            src_ref=bl.at[part], dst_ref=r1.at[m, part],
            send_sem=up_send, recv_sem=up_recv.at[group],
            device_id=line_peer(1), device_id_type=MESH,
        )

    def flat_copy(group, j):
        part = part_of[group]
        return pltpu.make_async_remote_copy(
            src_ref=r2.at[me, part], dst_ref=r2.at[me, part],
            send_sem=flat_send, recv_sem=flat_recv.at[group],
            device_id={"seq": (j // 8) * 24 + m, "grp": j % 8}, device_id_type=MESH,
        )

    def down_copy(group, j):
        part = part_of[group]
        return pltpu.make_async_remote_copy(
            src_ref=fin.at[part], dst_ref=fin.at[part],
            send_sem=down_send, recv_sem=down_recv,
            device_id=line_peer(j), device_id_type=MESH,
        )

    def bytes_of(ref, send_sem, recv_sem):
        return pltpu.make_async_remote_copy(
            src_ref=ref, dst_ref=ref, send_sem=send_sem, recv_sem=recv_sem,
            device_id=sib, device_id_type=MESH,
        )

    def send_up(group):
        @pl.when(adds)
        def _():
            r1[m, part_of[group]] = bl[part_of[group]]

        @pl.when(jnp.logical_not(adds))
        def _():
            up_copy(group).start()

    def add_line(group):
        part = part_of[group]
        bytes_of(r1.at[pl.ds(0, 23), part], up_send, up_recv.at[group]).wait_recv()
        r2[me, part] = jnp.sum(r1[:, part], axis=0)
        for j in order[:8]:

            @pl.when(me != j)
            def _(j=j):
                flat_copy(group, j).start()

    def add_plane(group):
        part = part_of[group]
        bytes_of(r2.at[pl.ds(0, 31), part], flat_send, flat_recv.at[group]).wait_recv()
        fin[part] = jnp.sum(r2[:, part], axis=0) * (n_seq * n_grp) ** (-0.5)
        for j in (0, *range(2, 6)):
            down_copy(group, j).start()

        @pl.when((me > 0) | (group == 0))
        def _():
            for j in range(6, 24):
                down_copy(group, j).start()

    both(arrive_lead)
    arrive_mixed()
    send_up(0)
    arrive_one(4)

    arrive_one(5)
    send_up(1)

    for h in (lack, 2):
        for part in range(2):
            pair_copy(h, part).start()
    for i in range(2):
        for part in range(2):
            second_copy(i, part).start()

    make_toep(e)

    def early(i, carry):
        h = jnp.where(i < 2, lead + i, 2 + i)
        outputs(d, h)
        return carry

    lax.fori_loop(0, 4, early, 0, unroll=2)

    @pl.when(adds)
    def _():
        for group in range(2):
            add_line(group)
        for j in order[8:]:

            @pl.when(me != j)
            def _(j=j):
                flat_copy(0, j).start()
                flat_copy(1, j).start()

    for h in (lack, 2):
        for part in range(2):
            pair_copy(h, part).wait_recv()
            relay_copy(h, part).start()
            relay_copy(h + 1, part).start()
    for h in (lack, lack + 1):
        scores(d, h, far_row(d), 128)
    for h in (lack, lack + 1, 2, 3):
        outputs(d, h)

    for i in range(2):
        heads = range(4 * i, 4 * i + 4)
        for part in range(2):
            for h in heads:
                relay_copy(h, part).wait_recv()
            second_copy(i, part).wait_recv()
        for h in heads:
            scores(e, h, 0, 384)
        for h in heads:
            outputs(e, h)
    for part in range(2):
        for rest in range(2):
            chip_copy(part, rest).wait_send()
        extra_copy(part).wait_send()

    @pl.when(c == 0)
    def _():
        mask_copy(0).wait_send()

    @pl.when(c == 1)
    def _():
        mask_copy(1).wait_send()

    def drain(h, carry):
        for part in range(2):
            relay_copy(h, part).wait_send()
        return carry

    lax.fori_loop(0, H, drain, 0)
    for part in range(2):
        for h in (lead, lead + 1, 4, 5):
            first_copy(h, part).wait_send()
        mixed_copy(part).wait_send()
        for h in (lack, 2):
            pair_copy(h, part).wait_send()
        for i in range(2):
            second_copy(i, part).wait_send()

    @pl.when(adds)
    def _():
        for group in range(2):
            add_plane(group)
        bytes_of(r2.at[pl.ds(0, 31)], flat_send, down_recv).wait_send()
        bytes_of(r1.at[pl.ds(0, 23), part_of[0]], down_send, down_recv).wait_send()
        bytes_of(r1.at[pl.ds(0, 5), part_of[1]], down_send, down_recv).wait_send()

        @pl.when(me > 0)
        def _():
            bytes_of(r1.at[pl.ds(0, 18), part_of[1]], down_send, down_recv).wait_send()

    @pl.when(jnp.logical_not(adds))
    def _():
        bytes_of(fin, up_send, down_recv).wait()

    @pl.when((m == 0) & (me == 0))
    def _():
        for j in range(6, 24):
            down_copy(1, j).start()
        bytes_of(r1.at[pl.ds(0, 18), part_of[1]], down_send, down_recv).wait_send()

    for h in range(H):
        for k in range(3):
            bg_ref[h : h + 1, 128 * k : 128 * k + 128] = fin[at[h] + k]


def copy_kernel(res_ref, bg_ref, att_ref, qg_ref, kg_ref, vg_ref, bias_ref, sem):
    copies = []
    for i, (side, part, ref) in enumerate(
        ((0, 0, att_ref), (0, 1, qg_ref), (1, 1, kg_ref), (1, 0, vg_ref))
    ):
        copy = pltpu.make_async_copy(res_ref.at[side, part], ref.at[0], sem.at[i])
        copy.start()
        copies.append(copy)
    copy = pltpu.make_async_copy(bg_ref, bias_ref, sem.at[4])
    copy.start()
    copies.append(copy)
    for copy in copies:
        copy.wait()


def on_device(queries, key_rows, value_rows, out_grad, positions, user_len, position_bias):
    hbm = pl.BlockSpec(memory_space=pltpu.HBM)
    vmem = pl.BlockSpec(memory_space=pltpu.VMEM)
    dma = pltpu.SemaphoreType.DMA
    res, bg = pl.pallas_call(
        main_kernel,
        out_shape=(
            jax.ShapeDtypeStruct((2, 2, BLOCK, D), BF16),
            jax.ShapeDtypeStruct((H, 384), F32),
        ),
        in_specs=[hbm] * 7,
        out_specs=(vmem, vmem),
        scratch_shapes=[
            pltpu.VMEM((2, 2, 384, D), BF16),
            pltpu.VMEM((2, 128, D), BF16),
            pltpu.VMEM((128, 256), F32),
            pltpu.VMEM((2, 128, 256), BF16),
            pltpu.VMEM((2, 128, 256), BF16),
            pltpu.VMEM((2, H, 128, 384), F32),
            pltpu.VMEM((2, 128, 384), F32),
            pltpu.VMEM((H, 384), F32),
            pltpu.SMEM((2, 1), jnp.int32),
            pltpu.VMEM((2, H, 128, 384), BF16),
            pltpu.VMEM((2, H, 128, 384), BF16),
            pltpu.VMEM((24, 1, 128), F32),
            pltpu.VMEM((24, 24, 1, 128), F32),
            pltpu.VMEM((32, 24, 1, 128), F32),
            pltpu.VMEM((24, 1, 128), F32),
            dma((4,)),
            dma((2, 2)),
            dma((2, 2)),
            dma((2,)),
            dma((2,)),
            dma(()),
            dma(()),
            dma((2,)),
            dma((2,)),
            dma((H, 2)),
            dma((H, 2)),
            dma((H, 2)),
            dma((H, 2)),
            dma((H, 2)),
            dma((H, 2)),
            dma(()),
            dma((3,)),
            dma(()),
            dma((3,)),
            dma(()),
            dma(()),
            dma((3,)),
        ],
        compiler_params=pltpu.CompilerParams(
            collective_id=0, has_side_effects=True, vmem_limit_bytes=32 * 1024 * 1024
        ),
        name="attention",
    )(*(pltpu.with_memory_space_constraint(a, pltpu.HBM) for a in (queries, key_rows, value_rows, out_grad)), positions, user_len, pltpu.with_memory_space_constraint(position_bias, pltpu.HBM))
    whole = jax.ShapeDtypeStruct((1, BLOCK, D), BF16)
    return pl.pallas_call(
        copy_kernel,
        out_shape=(whole, whole, whole, whole, jax.ShapeDtypeStruct((H, 384), F32)),
        in_specs=[vmem, vmem],
        out_specs=(hbm,) * 5,
        scratch_shapes=[dma((5,))],
        compiler_params=pltpu.CompilerParams(vmem_limit_bytes=4 * 1024 * 1024),
        name="results",
    )(res, bg)


def solution(mesh):
    return jax.shard_map(
        on_device,
        mesh=mesh,
        in_specs=(
            P("grp", "seq", None),
            P("grp", "seq", None),
            P("grp", "seq", None),
            P("grp", "seq", None),
            P("grp", "seq"),
            P("grp", "seq"),
            P(),
        ),
        out_specs=(
            P("grp", "seq", None),
            P("grp", "seq", None),
            P("grp", "seq", None),
            P("grp", "seq", None),
            P(),
        ),
        check_vma=False,
    )
```
